32 devices in a mesh: img: 2 (over x), tile: 16 (over z, y, core).
Axes of the slice: x: 2, y: 2, z: 4, core: 2. Of those that a mesh axis runs over, the one named last changes fastest.
Arguments:
- block_feature_map: bfloat16 [2, 192, 128, 256], P('img', None, 'tile'), may hold values from -12 to 12, as said below
- upstream_sensitivity: bfloat16 [2, 192, 128, 256], P('img', None, 'tile'), may hold values from -12 to 12, as said below
- triple_mixer: bfloat16 [576, 192], replicated, may hold values from -0.4375 to 0.4375
- spatial_stencil: float32 [576, 3, 3], replicated, may hold values from -2 to 2
- outgoing_mixer: bfloat16 [192, 192], replicated, may hold values from -0.4375 to 0.4375
- sharpness_factor: float32 [4], replicated, may hold values from 1 to 8
- standardize_scaling: float32 [192], replicated, may hold values from 0.5 to 1.5
- standardize_offset: float32 [192], replicated, may hold values from -1.5 to 1.5
Outputs:
- feature_map_adjoint: bfloat16 [2, 192, 128, 256], P('img', None, 'tile')
- triple_mixer_adjoint: float32 [576, 192], replicated
- spatial_stencil_adjoint: float32 [576, 3, 3], replicated
- outgoing_mixer_adjoint: float32 [192, 192], replicated
- sharpness_adjoint: float32 [4], replicated
- scaling_adjoint: float32 [192], replicated
- offset_adjoint: float32 [192], replicated
The draws below stay inside these ranges and needn't reach their ends.
Inputs may be any that keep to these rules, and one draw needn't show every extreme that they name: `block_feature_map`: the block's input feature map. `upstream_sensitivity`: gradient of the loss with respect to the block's output.
All inputs are finite; a program needn't handle non-finite values.
Results may differ from the reference program's by a relative error of at most 0.0072.
Values may be sent and summed in bfloat16 or wider, within the bound.
A program may use at most 64 MiB of HBM per device.

```python
import math
import jax
import jax.numpy as jnp
from jax import lax

C = 192
ATTN_GROUP_COUNT = 4
W = 256
H = 128
B = 2


def draw_block_feature_map(key, part):
    key_noise, key_slope = jax.random.split(jax.random.fold_in(key, 7), 2)
    row_place = 2.0 * jnp.arange(H, dtype=jnp.float32) / max(H - 1, 1) - 1.0
    slope = jax.random.uniform(key_slope, (C,), jnp.float32, -1.0, 1.0)
    channel_scale = jnp.exp(slope[:, None] * row_place[None, :] * math.log(3.0))
    noise = jnp.clip(jax.random.normal(key_noise, (B, C, H, W), jnp.float32), -4.0, 4.0)
    values = noise * channel_scale[None, :, :, None]
    return jnp.clip(values, -12.0, 12.0).astype(jnp.bfloat16)


def draw_upstream_sensitivity(key, part):
    key_noise, key_rows = jax.random.split(key, 2)
    row_place = jnp.arange(H, dtype=jnp.float32) / max(H - 1, 1)
    roughness = jax.random.uniform(key_rows, (H,), jnp.float32, 0.6, 1.4)
    row_scale = jnp.exp(row_place * math.log(3.0)) * roughness
    noise = jnp.clip(jax.random.normal(key_noise, (B, C, H, W), jnp.float32), -4.0, 4.0)
    return jnp.clip(noise * row_scale[None, None, :, None], -12.0, 12.0).astype(jnp.bfloat16)


def normal_values(key, dims, scale, limit, held_as=jnp.bfloat16):
    result = jax.random.normal(key, dims, jnp.float32) * scale
    return jnp.minimum(jnp.maximum(result, -limit), limit).astype(held_as)


def setup_inputs(seed: int = 0) -> dict:
    key_of = jax.random.split(jax.random.key(seed), 9)
    block_feature_map = draw_block_feature_map(jax.random.fold_in(key_of[8], 71), 0)
    upstream_sensitivity = draw_upstream_sensitivity(jax.random.fold_in(key_of[8], 71), 0)
    triple_mixer = normal_values(key_of[2], (3 * C, C), C ** -0.5, 0.4375)
    spatial_stencil = normal_values(key_of[3], (3 * C, 3, 3), 9 ** -0.5, 2.0, jnp.float32)
    outgoing_mixer = normal_values(key_of[4], (C, C), C ** -0.5, 0.4375)
    sharpness_factor = jnp.clip(jnp.exp(jax.random.uniform(key_of[5], (ATTN_GROUP_COUNT,), jnp.float32, math.log(1.0), math.log(8.0))), 1.0, 8.0)
    standardize_scaling = jnp.clip(1.0 + 0.1 * jax.random.normal(key_of[6], (C,), jnp.float32), 0.5, 1.5)
    standardize_offset = normal_values(key_of[7], (C,), 0.3, 1.5, jnp.float32)
    return {"block_feature_map": block_feature_map, "upstream_sensitivity": upstream_sensitivity, "triple_mixer": triple_mixer, "spatial_stencil": spatial_stencil, "outgoing_mixer": outgoing_mixer, "sharpness_factor": sharpness_factor, "standardize_scaling": standardize_scaling, "standardize_offset": standardize_offset}


def depthwise(padded, spatial_stencil):
    row_count = padded.shape[-2] - 2
    col_count = padded.shape[-1]
    widened = jnp.pad(padded.astype(jnp.float32), [(0, 0)] * (padded.ndim - 1) + [(1, 1)])
    summed = jnp.zeros(padded.shape[:-2] + (row_count, col_count), jnp.float32)
    for row_off in range(3):
        for col_off in range(3):
            summed = summed + spatial_stencil[:, row_off, col_off, None, None] * widened[..., row_off:row_off + row_count, col_off:col_off + col_count]
    return summed

def depthwise_back(padded, spatial_stencil):
    row_count = padded.shape[-2] - 2
    col_count = padded.shape[-1]
    widened = jnp.pad(padded.astype(jnp.float32), [(0, 0)] * (padded.ndim - 1) + [(1, 1)])
    summed = jnp.zeros(padded.shape[:-2] + (row_count, col_count), jnp.float32)
    for row_off in range(3):
        for col_off in range(3):
            summed = summed + spatial_stencil[:, row_off, col_off, None, None] * widened[..., 2 - row_off:2 - row_off + row_count, 2 - col_off:2 - col_off + col_count]
    return summed

def kernel_grad(grad_mixed, padded):
    row_count = grad_mixed.shape[-2]
    col_count = grad_mixed.shape[-1]
    grad_float = grad_mixed.astype(jnp.float32)
    widened = jnp.pad(padded.astype(jnp.float32), [(0, 0)] * (padded.ndim - 1) + [(1, 1)])
    reduce_axes = tuple((i for i in range(grad_mixed.ndim) if i != grad_mixed.ndim - 3))
    partials = []
    for row_off in range(3):
        for col_off in range(3):
            partials.append(lax.optimization_barrier(jnp.sum(grad_float * widened[..., row_off:row_off + row_count, col_off:col_off + col_count], axis=reduce_axes)))
    return jnp.stack(partials, axis=-1).reshape(grad_mixed.shape[-3], 3, 3)

def lone_sample(block_feature_map, upstream_sensitivity, triple_mixer, spatial_stencil, outgoing_mixer, sharpness_factor, standardize_scaling, standardize_offset):
    channels, row_count, col_count = block_feature_map.shape
    group_ordinal = sharpness_factor.shape[0]
    head_size = channels // group_ordinal
    pixel_count = row_count * col_count
    as_float = block_feature_map.astype(jnp.float32)
    average = lax.optimization_barrier(jnp.mean(as_float, axis=0, keepdims=True))
    centered = as_float - average
    inverse = lax.rsqrt(lax.optimization_barrier(jnp.mean(centered * centered, axis=0, keepdims=True)) + 1e-05)
    standard = centered * inverse
    normed = (standard * standardize_scaling[:, None, None] + standardize_offset[:, None, None]).astype(jnp.bfloat16)
    projected = jnp.einsum('oc,chw->ohw', triple_mixer.astype(jnp.float32), normed.astype(jnp.float32)).astype(jnp.bfloat16)
    padded = jnp.pad(projected, ((0, 0), (1, 1), (0, 0)))
    mixed = depthwise(padded, spatial_stencil).astype(jnp.bfloat16)
    query_part = mixed[:channels].reshape(group_ordinal, head_size, pixel_count).astype(jnp.float32)
    key_part = mixed[channels:2 * channels].reshape(group_ordinal, head_size, pixel_count).astype(jnp.float32)
    value_part = mixed[2 * channels:].reshape(group_ordinal, head_size, pixel_count).astype(jnp.float32)
    gram_raw = jnp.einsum('hip,hjp->hij', query_part, key_part)
    query_sq = lax.optimization_barrier(jnp.sum(query_part * query_part, axis=2))
    key_sq = lax.optimization_barrier(jnp.sum(key_part * key_part, axis=2))
    query_len = jnp.sqrt(query_sq + 1e-06)
    key_len = jnp.sqrt(key_sq + 1e-06)
    normalized_affinity = gram_raw / (query_len[:, :, None] * key_len[:, None, :])
    normalized_exp_logits = jnp.exp(normalized_affinity * sharpness_factor[:, None, None])
    attention = normalized_exp_logits / lax.optimization_barrier(jnp.sum(normalized_exp_logits, axis=2, keepdims=True))
    attention_b = attention.astype(jnp.bfloat16).astype(jnp.float32)
    attended = jnp.einsum('hij,hjp->hip', attention_b, value_part).astype(jnp.bfloat16)
    flat_out = attended.reshape(channels, pixel_count).astype(jnp.float32)
    flat_dy = upstream_sensitivity.reshape(channels, pixel_count).astype(jnp.float32)
    outgoing_mixer_adjoint = jnp.einsum('op,cp->oc', flat_dy, flat_out)
    grad_attended = jnp.einsum('oc,op->cp', outgoing_mixer.astype(jnp.float32), flat_dy).astype(jnp.bfloat16)
    grad_attended = grad_attended.reshape(group_ordinal, head_size, pixel_count).astype(jnp.float32)
    grad_attention = jnp.einsum('hip,hjp->hij', grad_attended, value_part)
    grad_value = jnp.einsum('hij,hip->hjp', attention_b, grad_attended)
    logits_adjoint = attention * (grad_attention - lax.optimization_barrier(jnp.sum(attention * grad_attention, axis=2, keepdims=True)))
    sharpness_adjoint = lax.optimization_barrier(jnp.sum(logits_adjoint * normalized_affinity, axis=(1, 2)))
    affinity_adjoint = logits_adjoint * sharpness_factor[:, None, None]
    grad_gram = (affinity_adjoint / (query_len[:, :, None] * key_len[:, None, :])).astype(jnp.bfloat16).astype(jnp.float32)
    product_terms = affinity_adjoint * normalized_affinity
    row_terms = lax.optimization_barrier(jnp.sum(product_terms, axis=2))
    col_terms = lax.optimization_barrier(jnp.sum(product_terms, axis=1))
    grad_query = jnp.einsum('hij,hjp->hip', grad_gram, key_part) - query_part * (row_terms / (query_sq + 1e-06))[:, :, None]
    grad_key = jnp.einsum('hij,hip->hjp', grad_gram, query_part) - key_part * (col_terms / (key_sq + 1e-06))[:, :, None]
    grad_mixed = jnp.concatenate([grad_query, grad_key, grad_value], axis=0).reshape(3 * channels, row_count, col_count).astype(jnp.bfloat16)
    grad_padded = jnp.pad(grad_mixed, ((0, 0), (1, 1), (0, 0)))
    grad_projected = depthwise_back(grad_padded, spatial_stencil).astype(jnp.bfloat16)
    spatial_stencil_adjoint = kernel_grad(grad_mixed, padded)
    flat_gproj = grad_projected.reshape(3 * channels, pixel_count).astype(jnp.float32)
    triple_mixer_adjoint = jnp.einsum('op,cp->oc', flat_gproj, normed.reshape(channels, pixel_count).astype(jnp.float32))
    grad_normed = jnp.einsum('oc,op->cp', triple_mixer.astype(jnp.float32), flat_gproj).reshape(channels, row_count, col_count)
    scaling_adjoint = lax.optimization_barrier(jnp.sum(grad_normed * standard, axis=(1, 2)))
    offset_adjoint = lax.optimization_barrier(jnp.sum(grad_normed, axis=(1, 2)))
    scaled = grad_normed * standardize_scaling[:, None, None]
    first_mean = lax.optimization_barrier(jnp.mean(scaled, axis=0, keepdims=True))
    second_mean = lax.optimization_barrier(jnp.mean(scaled * standard, axis=0, keepdims=True))
    feature_map_adjoint = (upstream_sensitivity.astype(jnp.float32) + (scaled - first_mean - standard * second_mean) * inverse).astype(jnp.bfloat16)
    return (feature_map_adjoint, triple_mixer_adjoint, spatial_stencil_adjoint, outgoing_mixer_adjoint, sharpness_adjoint, scaling_adjoint, offset_adjoint)

def reference(block_feature_map, upstream_sensitivity, triple_mixer, spatial_stencil, outgoing_mixer, sharpness_factor, standardize_scaling, standardize_offset):

    def per_image(paired_entries):
        return lone_sample(paired_entries[0], paired_entries[1], triple_mixer, spatial_stencil, outgoing_mixer, sharpness_factor, standardize_scaling, standardize_offset)
    results = lax.map(per_image, (block_feature_map, upstream_sensitivity))
    feature_map_adjoint = results[0]
    return (feature_map_adjoint, lax.optimization_barrier(jnp.sum(results[1], axis=0)), lax.optimization_barrier(jnp.sum(results[2], axis=0)), lax.optimization_barrier(jnp.sum(results[3], axis=0)), lax.optimization_barrier(jnp.sum(results[4], axis=0)), lax.optimization_barrier(jnp.sum(results[5], axis=0)), lax.optimization_barrier(jnp.sum(results[6], axis=0)))
```

```python
import functools
import jax
import jax.numpy as jnp
from jax import lax
from jax.experimental import pallas as pl
from jax.experimental.pallas import tpu as pltpu
from jax.sharding import PartitionSpec as P

F32 = jnp.float32
BF16 = jnp.bfloat16
NT = (((1,), (1,)), ((), ()))
NN = (((1,), (0,)), ((), ()))
TN = (((0,), (0,)), ((), ()))
VMEM = pl.BlockSpec(memory_space=pltpu.VMEM)
SMEM = pl.BlockSpec(memory_space=pltpu.SMEM)
LIMIT = 56 * 1024 * 1024


def dot(a, b, dims=NN):
    return lax.dot_general(a, b, dims, preferred_element_type=F32)


def standardized(x):
    xf = x.astype(F32)
    centered = xf - jnp.mean(xf, axis=0, keepdims=True)
    inverse = lax.rsqrt(jnp.mean(centered * centered, axis=0, keepdims=True) + 1e-05)
    return centered * inverse, inverse


def shifted(v, lanes):
    width = v.shape[-1]
    right = jnp.where(lanes == 0, 0.0, pltpu.roll(v, 1, 1))
    left = jnp.where(lanes == width - 1, 0.0, pltpu.roll(v, width - 1, 1))
    return right, left


def forward_kernel(
    lo_ref, own_ref, hi_ref, cot_ref, mixer_ref, stencil_ref, out_mixer_ref, scale_ref, offset_ref,
    flag_ref, mixed_ref, proj_ref, ga_ref, gram_ref, m_ref, acc_ref,
):
    rows, channels, width = own_ref.shape
    scale = scale_ref[...]
    offset = offset_ref[...]
    mixer = mixer_ref[...]
    out_mixer = out_mixer_ref[...]

    def project(x, flag):
        standard, _ = standardized(x)
        normed = (standard * scale + offset).astype(BF16)
        p = dot(mixer, normed)
        return (p if flag is None else p * flag).astype(BF16)

    for i in range(2):
        proj_ref[i] = project(lo_ref[i], flag_ref[0])
        proj_ref[rows + 2 + i] = project(hi_ref[i], flag_ref[1])

    @pl.loop(0, rows)
    def _(r):
        proj_ref[r + 2] = project(own_ref[r], None)

    ga_ref[0] = dot(out_mixer, lo_ref[2], TN).astype(BF16)
    ga_ref[rows + 1] = dot(out_mixer, hi_ref[2], TN).astype(BF16)

    @pl.loop(0, rows)
    def _(r):
        ga_ref[r + 1] = dot(out_mixer, cot_ref[r], TN).astype(BF16)

    group = 16
    lanes = lax.broadcasted_iota(jnp.int32, (group, width), 1)

    @pl.loop(0, 3 * channels // group)
    def _(g):
        at = pl.ds(pl.multiple_of(g * group, group), group)
        weights = stencil_ref[at, :]
        w = [jnp.broadcast_to(weights[:, t : t + 1], (group, width)) for t in range(9)]
        line = [proj_ref[i, at, :].astype(F32) for i in range(2)]
        for r in range(rows + 2):
            line.append(proj_ref[r + 2, at, :].astype(F32))
            sums = [
                w[b] * line[r] + w[3 + b] * line[r + 1] + w[6 + b] * line[r + 2] for b in range(3)
            ]
            right = jnp.where(lanes == 0, 0.0, pltpu.roll(sums[0], 1, 1))
            left = jnp.where(lanes == width - 1, 0.0, pltpu.roll(sums[2], width - 1, 1))
            mixed_ref[r, at, :] = (sums[1] + right + left).astype(BF16)

    acc_ref[...] = jnp.zeros_like(acc_ref)

    @pl.loop(0, rows)
    def _(r):
        q = mixed_ref[r + 1, 0:channels, :]
        k = mixed_ref[r + 1, channels : 2 * channels, :]
        v = mixed_ref[r + 1, 2 * channels : 3 * channels, :]
        acc_ref[0] += dot(q, k, NT)
        acc_ref[1] += dot(ga_ref[r + 1], v, NT)
        acc_ref[2] += dot(cot_ref[r], v, NT)
        qf = q.astype(F32)
        kf = k.astype(F32)
        acc_ref[3, :, 0:1] += jnp.sum(qf * qf, axis=1, keepdims=True)
        acc_ref[3, :, 1:2] += jnp.sum(kf * kf, axis=1, keepdims=True)

    m_ref[...] = acc_ref[2]
    gram_ref[...] = jnp.zeros_like(gram_ref)
    heads = channels // 48
    for h in range(heads):
        a, b = 48 * h, 48 * (h + 1)
        gram_ref[a:b, 0:48] = acc_ref[0, a:b, a:b]
        gram_ref[a:b, 48:96] = acc_ref[1, a:b, a:b]
    gram_ref[0:channels, 96:98] = acc_ref[3, :, 0:2]


def backward_kernel(
    mixed_ref, proj_ref, ga_ref, gram_ref, m_ref, own_ref, cot_ref, mixer_ref, stencil_ref,
    scale_ref, sharp_ref, flag_ref, out_ref, red_ref, gg_ref, ggt_ref, at_ref, coef_ref,
    gm_ref, gp_ref, sacc_ref, extra_ref,
):
    rows, channels, width = own_ref.shape
    heads = channels // 48
    gg_ref[...] = jnp.zeros_like(gg_ref)
    ggt_ref[...] = jnp.zeros_like(ggt_ref)
    at_ref[...] = jnp.zeros_like(at_ref)
    extra_ref[...] = jnp.zeros_like(extra_ref)
    sacc_ref[...] = jnp.zeros_like(sacc_ref)
    eye = lax.broadcasted_iota(jnp.int32, (48, 48), 0) == lax.broadcasted_iota(
        jnp.int32, (48, 48), 1
    )
    lane = lax.broadcasted_iota(jnp.int32, (1, 128), 1)
    for h in range(heads):
        a, b = 48 * h, 48 * (h + 1)
        gram = gram_ref[a:b, 0:48]
        grad_att = gram_ref[a:b, 48:96]
        qsq = gram_ref[a:b, 96:97]
        ksq_col = gram_ref[a:b, 97:98]
        ksq = jnp.sum(jnp.where(eye, ksq_col, 0.0), axis=0, keepdims=True)
        lengths = jnp.sqrt(qsq + 1e-06) * jnp.sqrt(ksq + 1e-06)
        cosine = gram / lengths
        e = jnp.exp(cosine * sharp_ref[h])
        attention = e / jnp.sum(e, axis=1, keepdims=True)
        grad_scores = attention * (grad_att - jnp.sum(attention * grad_att, axis=1, keepdims=True))
        sharp_sum = jnp.sum(jnp.sum(grad_scores * cosine, axis=1, keepdims=True), axis=0, keepdims=True)
        sharp_sum = sharp_sum * flag_ref[2]
        sharp_hi = sharp_sum.astype(BF16).astype(F32)
        extra_ref[3 * channels : 3 * channels + 1, :] += jnp.where(lane == 64 + h, sharp_hi, 0.0)
        extra_ref[3 * channels : 3 * channels + 1, :] += jnp.where(
            lane == 68 + h, sharp_sum - sharp_hi, 0.0
        )
        grad_cos = grad_scores * sharp_ref[h]
        gg = grad_cos / lengths
        terms = grad_cos * cosine
        gg_ref[a:b, a:b] = gg.astype(BF16)
        ggt_ref[a:b, a:b] = gg.T.astype(BF16)
        at_ref[a:b, a:b] = attention.T.astype(BF16)
        coef_ref[a:b, 0:1] = jnp.sum(terms, axis=1, keepdims=True) / (qsq + 1e-06)
        kc = jnp.sum(terms, axis=0, keepdims=True) / (ksq + 1e-06)
        coef_ref[a:b, 1:2] = jnp.sum(jnp.where(eye, kc, 0.0), axis=1, keepdims=True)

    oma = dot(m_ref[...].astype(BF16), at_ref[...])

    qc = coef_ref[:, 0:1]
    kc = coef_ref[:, 1:2]

    def grads(r, flag):
        q = mixed_ref[r, 0:channels, :]
        k = mixed_ref[r, channels : 2 * channels, :]
        gq = dot(gg_ref[...], k) - q.astype(F32) * qc
        gk = dot(ggt_ref[...], q) - k.astype(F32) * kc
        gv = dot(at_ref[...], ga_ref[r])
        if flag is not None:
            gq, gk, gv = gq * flag, gk * flag, gv * flag
        gm_ref[r, 0:channels, :] = gq.astype(BF16)
        gm_ref[r, channels : 2 * channels, :] = gk.astype(BF16)
        gm_ref[r, 2 * channels : 3 * channels, :] = gv.astype(BF16)

    grads(0, flag_ref[0])
    grads(rows + 1, flag_ref[1])

    @pl.loop(1, rows + 1)
    def _(r):
        grads(r, None)

    group = 16
    lanes = lax.broadcasted_iota(jnp.int32, (group, width), 1)
    lane_g = lax.broadcasted_iota(jnp.int32, (group, 128), 1)

    @pl.loop(0, 3 * channels // group)
    def _(g):
        at = pl.ds(pl.multiple_of(g * group, group), group)
        weights = stencil_ref[at, :]
        w = [jnp.broadcast_to(weights[:, t : t + 1], (group, width)) for t in range(9)]
        line = [gm_ref[i, at, :].astype(F32) for i in range(2)]
        for r in range(rows):
            line.append(gm_ref[r + 2, at, :].astype(F32))
            sums = [
                w[b] * line[r + 2] + w[3 + b] * line[r + 1] + w[6 + b] * line[r] for b in range(3)
            ]
            left = jnp.where(lanes == width - 1, 0.0, pltpu.roll(sums[0], width - 1, 1))
            right = jnp.where(lanes == 0, 0.0, pltpu.roll(sums[2], 1, 1))
            gp_ref[r, at, :] = (sums[1] + right + left).astype(BF16)

    @pl.loop(0, 3 * channels // group)
    def _(g):
        at = pl.ds(pl.multiple_of(g * group, group), group)
        acc = [jnp.zeros((group, width), F32) for _ in range(9)]
        for r in range(rows):
            g_mid = gm_ref[r + 1, at, :].astype(F32)
            right, left = shifted(g_mid, lanes)
            for a in range(3):
                p = proj_ref[r + 1 + a, at, :].astype(F32)
                acc[3 * a] += p * left
                acc[3 * a + 1] += p * g_mid
                acc[3 * a + 2] += p * right
        total = jnp.zeros((group, 128), F32)
        for t in range(9):
            s = jnp.sum(acc[t], axis=1, keepdims=True)
            total = total + jnp.where(lane_g == 72 + t, s, 0.0)
        extra_ref[at, :] = total

    scale = scale_ref[...]
    mixer = mixer_ref[...]

    @pl.loop(0, rows)
    def _(r):
        standard, inverse = standardized(own_ref[r])
        gp = gp_ref[r]
        right = jnp.concatenate([standard.astype(BF16), jnp.ones((64, width), BF16)], axis=0)
        sacc_ref[...] += dot(gp, right, NT)
        scaled = dot(mixer, gp, TN) * scale
        first = jnp.mean(scaled, axis=0, keepdims=True)
        second = jnp.mean(scaled * standard, axis=0, keepdims=True)
        out_ref[r] = (
            cot_ref[r].astype(F32) + (scaled - first - standard * second) * inverse
        ).astype(BF16)

    n1 = 3 * channels
    n2 = 4 * channels
    red_ref[0:n1, :] = sacc_ref[:, 0:128].astype(BF16)
    red_ref[n1:n2, :] = oma[:, 0:128].astype(BF16)
    tail = sacc_ref[:, 128:256]
    tail_lane = lax.broadcasted_iota(jnp.int32, tail.shape, 1)
    hi = tail.astype(BF16).astype(F32)
    tail = jnp.where(tail_lane <= 64, tail, jnp.where(tail_lane == 65, tail - hi, 0.0))
    red_ref[n2 : n2 + n1, :] = (tail + extra_ref[0:n1, :]).astype(BF16)
    oma_tail = jnp.concatenate([oma[:, 128:192], jnp.zeros((channels, 64), F32)], axis=1)
    red_ref[n2 + n1 :, :] = (oma_tail + extra_ref[n1:, :]).astype(BF16)


def reduce_kernel(axes, src_ref, out_ref, recv, gath, send1, recv1, send2, recv2):
    n = src_ref.shape[0]
    me = jnp.int32(0)
    for name, size in axes:
        me = me * size + lax.axis_index(name)

    def device(p):
        ids = {}
        for name, size in reversed(axes):
            ids[name] = lax.rem(p, size)
            p = lax.div(p, size)
        return ids

    def peer(d):
        return lax.rem(me + d, n)

    barrier = pltpu.get_barrier_semaphore()

    @pl.loop(1, n)
    def _(d):
        pl.semaphore_signal(
            barrier, inc=1, device_id=device(peer(d)), device_id_type=pl.DeviceIdType.MESH
        )

    pl.semaphore_wait(barrier, n - 1)

    @pl.loop(1, n)
    def _(d):
        p = peer(d)
        pltpu.make_async_remote_copy(
            src_ref=src_ref.at[p], dst_ref=recv.at[me], send_sem=send1, recv_sem=recv1,
            device_id=device(p), device_id_type=pl.DeviceIdType.MESH,
        ).start()

    recv[me] = src_ref[me]
    all_but_one = pl.ds(0, n - 1)
    pltpu.make_async_copy(recv.at[all_but_one], recv.at[all_but_one], recv1).wait()

    def add(i, acc):
        return acc + recv[i].astype(F32)

    total = lax.fori_loop(0, n, add, jnp.zeros(src_ref.shape[1:], F32))
    gath[me] = total.astype(gath.dtype)

    @pl.loop(1, n)
    def _(d):
        p = peer(d)
        pltpu.make_async_remote_copy(
            src_ref=gath.at[me], dst_ref=gath.at[me], send_sem=send2, recv_sem=recv2,
            device_id=device(p), device_id_type=pl.DeviceIdType.MESH,
        ).start()

    pltpu.make_async_copy(gath.at[all_but_one], gath.at[all_but_one], recv2).wait()
    out_ref[...] = gath[...]
    pltpu.make_async_copy(gath.at[all_but_one], gath.at[all_but_one], send2).wait()
    pltpu.make_async_copy(recv.at[all_but_one], recv.at[all_but_one], send1).wait()


def all_reduce(x, axes, tile_rows, collective_id):
    axes = tuple((name, lax.axis_size(name)) for name in axes)
    n = 1
    for _, size in axes:
        n *= size
    rows = x.shape[0]
    each = -(-rows // (n * tile_rows)) * tile_rows
    if each * n != rows:
        x = jnp.pad(x, ((0, each * n - rows), (0, 0)))
    x = x.reshape(n, each, 128)
    slots = pltpu.VMEM((n, each, 128), x.dtype)
    sem = pltpu.SemaphoreType.DMA
    out = pl.pallas_call(
        functools.partial(reduce_kernel, axes),
        out_shape=jax.ShapeDtypeStruct(x.shape, x.dtype),
        in_specs=[VMEM],
        out_specs=VMEM,
        scratch_shapes=[slots, slots, sem, sem, sem, sem],
        compiler_params=pltpu.CompilerParams(
            collective_id=collective_id, has_side_effects=True, vmem_limit_bytes=LIMIT
        ),
        name=f"all_reduce_{collective_id}",
    )(x)
    return out.reshape(n * each, 128)[:rows]


def local(
    block_feature_map, upstream_sensitivity, triple_mixer, spatial_stencil, outgoing_mixer,
    sharpness_factor, standardize_scaling, standardize_offset,
):
    _, channels, rows, width = block_feature_map.shape
    heads = sharpness_factor.shape[0]
    n = lax.axis_size("tile")
    me = lax.axis_index("tile")
    own = jnp.transpose(block_feature_map[0], (1, 0, 2))
    cot = jnp.transpose(upstream_sensitivity[0], (1, 0, 2))
    up = [(i, i + 1) for i in range(n - 1)]
    down = [(j, i) for i, j in up]
    last = jnp.concatenate([own[rows - 2 :], cot[rows - 1 :]], axis=0)
    first = jnp.concatenate([own[:2], cot[:1]], axis=0)
    lo = lax.ppermute(last, "tile", up)
    hi = lax.ppermute(first, "tile", down)
    flags = jnp.stack([me > 0, me < n - 1, me == 0]).astype(F32)
    stencil = spatial_stencil.reshape(3 * channels, 9)
    scale = standardize_scaling.reshape(channels, 1)
    offset = standardize_offset.reshape(channels, 1)

    params = pltpu.CompilerParams(vmem_limit_bytes=LIMIT)
    shape = jax.ShapeDtypeStruct
    mixed, proj, ga, gram, m = pl.pallas_call(
        forward_kernel,
        out_shape=(
            shape((rows + 2, 3 * channels, width), BF16),
            shape((rows + 4, 3 * channels, width), BF16),
            shape((rows + 2, channels, width), BF16),
            shape((channels, 128), F32),
            shape((channels, channels), F32),
        ),
        in_specs=[VMEM] * 9 + [SMEM],
        out_specs=[VMEM] * 5,
        scratch_shapes=[pltpu.VMEM((4, channels, channels), F32)],
        compiler_params=params,
        name="forward",
    )(lo, own, hi, cot, triple_mixer, stencil, outgoing_mixer, scale, offset, flags)

    gram = all_reduce(gram, ("tile",), 8, 1)

    out, red = pl.pallas_call(
        backward_kernel,
        out_shape=(
            shape((rows, channels, width), BF16),
            shape((8 * channels, 128), BF16),
        ),
        in_specs=[VMEM] * 10 + [SMEM] * 2,
        out_specs=[VMEM] * 2,
        scratch_shapes=[
            pltpu.VMEM((channels, channels), BF16),
            pltpu.VMEM((channels, channels), BF16),
            pltpu.VMEM((channels, channels), BF16),
            pltpu.VMEM((channels, 128), F32),
            pltpu.VMEM((rows + 2, 3 * channels, width), BF16),
            pltpu.VMEM((rows, 3 * channels, width), BF16),
            pltpu.VMEM((3 * channels, 256), F32),
            pltpu.VMEM((4 * channels, 128), F32),
        ],
        compiler_params=params,
        name="backward",
    )(mixed, proj, ga, gram, m, own, cot, triple_mixer, stencil, scale, sharpness_factor, flags)

    red = all_reduce(red, ("img", "tile"), 16, 2).astype(F32)
    n1 = 3 * channels
    left, right = red[: 4 * channels], red[4 * channels :]
    s = jnp.concatenate([left[:n1], right[:n1, :64]], axis=1)
    gsum = right[:n1, 64:65] + right[:n1, 65:66]
    triple_adjoint = s * standardize_scaling[None, :] + gsum * standardize_offset[None, :]
    mixer = triple_mixer.astype(F32)
    return (
        jnp.transpose(out, (1, 0, 2))[None],
        triple_adjoint,
        right[:n1, 72:81].reshape(n1, 3, 3),
        jnp.concatenate([left[n1:], right[n1:, :64]], axis=1),
        right[n1, 64 : 64 + heads] + right[n1, 68 : 68 + heads],
        jnp.sum(mixer * s, axis=0),
        jnp.sum(mixer * gsum, axis=0),
    )


def solution(mesh):
    rows = P("img", None, "tile", None)
    return jax.shard_map(
        local,
        mesh=mesh,
        in_specs=(rows, rows, P(), P(), P(), P(), P(), P()),
        out_specs=(rows, P(), P(), P(), P(), P(), P()),
        check_vma=False,
    )
```

```python
import functools
import jax
import jax.numpy as jnp
from jax import lax
from jax.experimental import pallas as pl
from jax.experimental.pallas import tpu as pltpu
from jax.sharding import PartitionSpec as P

F32 = jnp.float32
BF16 = jnp.bfloat16
NT = (((1,), (1,)), ((), ()))
NN = (((1,), (0,)), ((), ()))
TN = (((0,), (0,)), ((), ()))
VMEM = pl.BlockSpec(memory_space=pltpu.VMEM)
SMEM = pl.BlockSpec(memory_space=pltpu.SMEM)
LIMIT = 56 * 1024 * 1024


def dot(a, b, dims=NN):
    return lax.dot_general(a, b, dims, preferred_element_type=F32)


def standardized(x):
    xf = x.astype(F32)
    centered = xf - jnp.mean(xf, axis=0, keepdims=True)
    inverse = lax.rsqrt(jnp.mean(centered * centered, axis=0, keepdims=True) + 1e-05)
    return centered * inverse, inverse


def shifted(v, lanes):
    width = v.shape[-1]
    right = jnp.where(lanes == 0, 0.0, pltpu.roll(v, 1, 1))
    left = jnp.where(lanes == width - 1, 0.0, pltpu.roll(v, width - 1, 1))
    return right, left


def column(row):
    n = row.shape[1]
    eye = lax.broadcasted_iota(jnp.int32, (n, n), 0) == lax.broadcasted_iota(jnp.int32, (n, n), 1)
    return jnp.sum(jnp.where(eye, row, 0.0), axis=1, keepdims=True)


def remote(src, dst, sems, ids):
    return pltpu.make_async_remote_copy(
        src_ref=src, dst_ref=dst, send_sem=sems.at[0], recv_sem=sems.at[1], device_id=ids,
        device_id_type=pl.DeviceIdType.MESH,
    )


def wait_bytes(ref, sem):
    pltpu.make_async_copy(ref, ref, sem).wait()


def kernel(
    n_img, n_tile,
    own_ref, cot_ref, mixer_ref, stencil_ref, out_mixer_ref, scale_ref, offset_ref, sharp_ref,
    out_ref, triple_ref, stencil_out_ref, outgoing_ref, sharp_out_ref, scaling_ref, offset_out_ref,
    lo, hi, proj, mixed, ga, gm, gp, acc, gram, gram_recv, gram_all, gg_ref, ggt_ref, at_ref, coef,
    sacc, extra, red, pair, half, recv, gath,
    lo_x, lo_c, hi_x, hi_c, gram_rs, gram_ag, pair_rs, main_rs, main_ag, pair_ag,
):
    rows, channels, width = own_ref.shape
    heads = channels // 48
    img = lax.axis_index("img")
    tile = lax.axis_index("tile")
    n = n_img * n_tile
    me = img * n_tile + tile

    def device(p):
        return {"img": lax.div(p, n_tile), "tile": lax.rem(p, n_tile)}

    barrier = pltpu.get_barrier_semaphore()

    @pl.loop(1, n)
    def _(d):
        pl.semaphore_signal(
            barrier, inc=1, device_id=device(lax.rem(me + d, n)),
            device_id_type=pl.DeviceIdType.MESH,
        )

    pl.semaphore_wait(barrier, n - 1)

    def to_next():
        ids = {"img": img, "tile": tile + 1}
        return (
            remote(own_ref.at[pl.ds(rows - 2, 2)], lo.at[pl.ds(0, 2)], lo_x, ids),
            remote(cot_ref.at[pl.ds(rows - 1, 1)], lo.at[pl.ds(2, 1)], lo_c, ids),
        )

    def to_previous():
        ids = {"img": img, "tile": tile - 1}
        return (
            remote(own_ref.at[pl.ds(0, 2)], hi.at[pl.ds(0, 2)], hi_x, ids),
            remote(cot_ref.at[pl.ds(0, 1)], hi.at[pl.ds(2, 1)], hi_c, ids),
        )

    has_lo = tile > 0
    has_hi = tile < n_tile - 1

    @pl.when(has_hi)
    def _():
        for copy in to_next():
            copy.start()

    @pl.when(has_lo)
    def _():
        for copy in to_previous():
            copy.start()

    scale = column(scale_ref[...])
    offset = column(offset_ref[...])
    mixer = mixer_ref[...]
    out_mixer = out_mixer_ref[...]

    def project(x):
        standard, _ = standardized(x)
        normed = (standard * scale + offset).astype(BF16)
        return dot(mixer, normed).astype(BF16)

    @pl.loop(0, rows, unroll=2)
    def _(r):
        proj[r + 2] = project(own_ref[r])
        ga[r + 1] = dot(out_mixer, cot_ref[r], TN).astype(BF16)

    @pl.when(has_lo)
    def _():
        for copy in to_next():
            copy.wait_recv()
        for i in range(2):
            proj[i] = project(lo[i])
        ga[0] = dot(out_mixer, lo[2], TN).astype(BF16)

    @pl.when(jnp.logical_not(has_lo))
    def _():
        proj[0:2] = jnp.zeros((2,) + proj.shape[1:], BF16)
        ga[0] = jnp.zeros(ga.shape[1:], BF16)

    @pl.when(has_hi)
    def _():
        for copy in to_previous():
            copy.wait_recv()
        for i in range(2):
            proj[rows + 2 + i] = project(hi[i])
        ga[rows + 1] = dot(out_mixer, hi[2], TN).astype(BF16)

    @pl.when(jnp.logical_not(has_hi))
    def _():
        proj[rows + 2 : rows + 4] = jnp.zeros((2,) + proj.shape[1:], BF16)
        ga[rows + 1] = jnp.zeros(ga.shape[1:], BF16)

    group = 16
    lanes = lax.broadcasted_iota(jnp.int32, (group, width), 1)

    @pl.loop(0, 3 * channels // group)
    def _(g):
        at = pl.ds(pl.multiple_of(g * group, group), group)
        weights = stencil_ref[at, :]
        w = [jnp.broadcast_to(weights[:, t : t + 1], (group, width)) for t in range(9)]
        line = [proj[i, at, :].astype(F32) for i in range(2)]
        for r in range(rows + 2):
            line.append(proj[r + 2, at, :].astype(F32))
            sums = [
                w[b] * line[r] + w[3 + b] * line[r + 1] + w[6 + b] * line[r + 2] for b in range(3)
            ]
            right = jnp.where(lanes == 0, 0.0, pltpu.roll(sums[0], 1, 1))
            left = jnp.where(lanes == width - 1, 0.0, pltpu.roll(sums[2], width - 1, 1))
            mixed[r, at, :] = (sums[1] + right + left).astype(BF16)

    acc[...] = jnp.zeros_like(acc)

    @pl.loop(0, rows, unroll=2)
    def _(r):
        q = mixed[r + 1, 0:channels, :]
        k = mixed[r + 1, channels : 2 * channels, :]
        v = mixed[r + 1, 2 * channels : 3 * channels, :]
        acc[0, :, 0:channels] += dot(q, k, NT)
        acc[1, :, 0:channels] += dot(ga[r + 1], v, NT)
        acc[2, :, 0:channels] += dot(cot_ref[r], v, NT)
        qf = q.astype(F32)
        kf = k.astype(F32)
        acc[3] += qf * qf
        acc[4] += kf * kf

    each = gram.shape[1]
    owners = gram.shape[0]
    gram_rows = owners * each
    pieces = []
    for h in range(heads):
        a, b = 48 * h, 48 * (h + 1)
        qsq = jnp.sum(acc[3, a:b, :], axis=1, keepdims=True)
        ksq = jnp.sum(acc[4, a:b, :], axis=1, keepdims=True)
        pieces.append(
            jnp.concatenate(
                [acc[0, a:b, a:b], acc[1, a:b, a:b], qsq, ksq, jnp.zeros((48, 30), F32)], axis=1,
            )
        )
    if gram_rows > channels:
        pieces.append(jnp.zeros((gram_rows - channels, 128), F32))
    packed = jnp.concatenate(pieces, axis=0)
    for i in range(owners):
        gram[i] = packed[i * each : (i + 1) * each]

    owner = tile < owners
    rest = pl.ds(0, n_tile - 1)

    @pl.loop(1, n_tile)
    def _(d):
        p = lax.rem(tile + d, n_tile)

        @pl.when(p < owners)
        def _():
            remote(gram.at[p], gram_recv.at[tile], gram_rs, {"img": img, "tile": p}).start()

    @pl.when(owner)
    def _():
        gram_recv[tile] = gram[tile]
        wait_bytes(gram_recv.at[rest], gram_rs.at[1])

        def add_gram(i, total):
            return total + gram_recv[i]

        gram_all[tile] = lax.fori_loop(0, n_tile, add_gram, jnp.zeros(gram.shape[1:], F32))

        @pl.loop(1, n_tile)
        def _(d):
            p = lax.rem(tile + d, n_tile)
            remote(gram_all.at[tile], gram_all.at[tile], gram_ag, {"img": img, "tile": p}).start()

    gg_ref[...] = jnp.zeros_like(gg_ref)
    ggt_ref[...] = jnp.zeros_like(ggt_ref)
    at_ref[...] = jnp.zeros_like(at_ref)
    extra[...] = jnp.zeros_like(extra)
    sacc[...] = jnp.zeros_like(sacc)

    @pl.when(owner)
    def _():
        wait_bytes(gram_all.at[pl.ds(0, owners - 1)], gram_ag.at[1])

    @pl.when(jnp.logical_not(owner))
    def _():
        wait_bytes(gram_all, gram_ag.at[1])

    whole = jnp.concatenate([gram_all[i] for i in range(owners)], axis=0)

    eye = lax.broadcasted_iota(jnp.int32, (48, 48), 0) == lax.broadcasted_iota(
        jnp.int32, (48, 48), 1
    )
    lane = lax.broadcasted_iota(jnp.int32, (1, 128), 1)
    leading = (tile == 0).astype(F32)
    for h in range(heads):
        a, b = 48 * h, 48 * (h + 1)
        gram_raw = whole[a:b, 0:48]
        grad_att = whole[a:b, 48:96]
        qsq = whole[a:b, 96:97]
        ksq_col = whole[a:b, 97:98]
        ksq = jnp.sum(jnp.where(eye, ksq_col, 0.0), axis=0, keepdims=True)
        lengths = jnp.sqrt(qsq + 1e-06) * jnp.sqrt(ksq + 1e-06)
        cosine = gram_raw / lengths
        e = jnp.exp(cosine * sharp_ref[h])
        attention = e / jnp.sum(e, axis=1, keepdims=True)
        grad_scores = attention * (grad_att - jnp.sum(attention * grad_att, axis=1, keepdims=True))
        sharp_sum = leading * jnp.sum(
            jnp.sum(grad_scores * cosine, axis=1, keepdims=True), axis=0, keepdims=True
        )
        extra[3 * channels : 3 * channels + 1, :] += jnp.where(lane == 64 + h, sharp_sum, 0.0)
        grad_cos = grad_scores * sharp_ref[h]
        gg = grad_cos / lengths
        terms = grad_cos * cosine
        gg_ref[a:b, a:b] = gg.astype(BF16)
        ggt_ref[a:b, a:b] = gg.T.astype(BF16)
        at_ref[a:b, a:b] = attention.T.astype(BF16)
        coef[a:b, 0:1] = jnp.sum(terms, axis=1, keepdims=True) / (qsq + 1e-06)
        kc = jnp.sum(terms, axis=0, keepdims=True) / (ksq + 1e-06)
        coef[a:b, 1:2] = jnp.sum(jnp.where(eye, kc, 0.0), axis=1, keepdims=True)

    oma = dot(acc[2, :, 0:channels].astype(BF16), at_ref[...])

    qc = coef[:, 0:1]
    kc = coef[:, 1:2]

    @pl.loop(0, rows + 2, unroll=2)
    def _(r):
        inside = jnp.logical_and(
            jnp.logical_or(r > 0, has_lo), jnp.logical_or(r < rows + 1, has_hi)
        ).astype(F32)
        q = mixed[r, 0:channels, :]
        k = mixed[r, channels : 2 * channels, :]
        gq = dot(gg_ref[...], k) - q.astype(F32) * qc
        gk = dot(ggt_ref[...], q) - k.astype(F32) * kc
        gv = dot(at_ref[...], ga[r])
        gm[r, 0:channels, :] = (gq * inside).astype(BF16)
        gm[r, channels : 2 * channels, :] = (gk * inside).astype(BF16)
        gm[r, 2 * channels : 3 * channels, :] = (gv * inside).astype(BF16)

    lane_g = lax.broadcasted_iota(jnp.int32, (group, 128), 1)

    @pl.loop(0, 3 * channels // group)
    def _(g):
        at = pl.ds(pl.multiple_of(g * group, group), group)
        weights = stencil_ref[at, :]
        w = [jnp.broadcast_to(weights[:, t : t + 1], (group, width)) for t in range(9)]
        line = [gm[i, at, :].astype(F32) for i in range(2)]
        for r in range(rows):
            line.append(gm[r + 2, at, :].astype(F32))
            sums = [
                w[b] * line[r + 2] + w[3 + b] * line[r + 1] + w[6 + b] * line[r] for b in range(3)
            ]
            left = jnp.where(lanes == width - 1, 0.0, pltpu.roll(sums[0], width - 1, 1))
            right = jnp.where(lanes == 0, 0.0, pltpu.roll(sums[2], 1, 1))
            gp[r, at, :] = (sums[1] + right + left).astype(BF16)

    @pl.loop(0, 3 * channels // group)
    def _(g):
        at = pl.ds(pl.multiple_of(g * group, group), group)
        tap = [jnp.zeros((group, width), F32) for _ in range(9)]
        line = [proj[1 + i, at, :].astype(F32) for i in range(2)]
        for r in range(rows):
            line.append(proj[r + 3, at, :].astype(F32))
            g_mid = gm[r + 1, at, :].astype(F32)
            right, left = shifted(g_mid, lanes)
            for a in range(3):
                tap[3 * a] += line[r + a] * left
                tap[3 * a + 1] += line[r + a] * g_mid
                tap[3 * a + 2] += line[r + a] * right
        total = jnp.zeros((group, 128), F32)
        for t in range(9):
            s = jnp.sum(tap[t], axis=1, keepdims=True)
            total = total + jnp.where(lane_g == 72 + t, s, 0.0)
        extra[at, :] = total

    @pl.loop(0, rows, unroll=2)
    def _(r):
        standard, _ = standardized(own_ref[r])
        ext = jnp.concatenate([standard.astype(BF16), jnp.ones((64, width), BF16)], axis=0)
        sacc[...] += dot(gp[r], ext, NT)

    n1 = 3 * channels
    n2 = 4 * channels
    groups, piece = half.shape[:2]
    tail = sacc[:, 128:256]
    tail_lane = lax.broadcasted_iota(jnp.int32, tail.shape, 1)
    tail = jnp.where(tail_lane <= 64, tail, 0.0)
    mixer_f = mixer_ref[...].astype(F32)
    scaling_part = jnp.sum(mixer_f * sacc[:, 0:channels], axis=0, keepdims=True)
    oma_lane = lax.broadcasted_iota(jnp.int32, (channels, 128), 1)
    oma_tail = jnp.concatenate([oma[:, 128:192], jnp.zeros((channels, 64), F32)], axis=1)
    oma_tail = oma_tail + jnp.where(oma_lane == 72, column(scaling_part), 0.0)

    def split_again(x):
        at = lax.broadcasted_iota(jnp.int32, x.shape, x.ndim - 1)
        both = x + pltpu.roll(x, 96, x.ndim - 1)
        high = both.astype(BF16).astype(F32)
        low = pltpu.roll(both - high, 32, x.ndim - 1)
        return jnp.where(at < 64, x, jnp.where(at < 96, high, low))

    spare = groups * piece - n2
    filler = [jnp.zeros((spare, 128), BF16)] if spare else []
    head_part = [sacc[:, 0:128].astype(BF16), oma[:, 0:128].astype(BF16)] + filler
    tail_part = [
        split_again(tail + extra[0:n1, :]).astype(BF16),
        split_again(oma_tail + extra[n1:, :]).astype(BF16),
    ] + filler
    red[0] = jnp.concatenate(head_part, axis=0).reshape(half.shape)
    red[1] = jnp.concatenate(tail_part, axis=0).reshape(half.shape)

    core = lax.rem(tile, 2)
    place = lax.div(me, 2)
    partner = {"img": img, "tile": tile + 1 - 2 * core}
    others = pl.ds(0, groups - 1)

    swap = remote(red.at[1 - core], pair, pair_rs, partner)
    swap.start()
    swap.wait_recv()

    def rounded(x):
        return jnp.where(core == 1, split_again(x), x).astype(BF16)

    def add_pair(i, _):
        half[i] = rounded(red[core, i].astype(F32) + pair[i].astype(F32))
        return 0

    lax.fori_loop(0, groups, add_pair, 0)

    @pl.loop(1, groups)
    def _(d):
        p = lax.rem(place + d, groups)
        remote(half.at[p], recv.at[place], main_rs, device(2 * p + core)).start()

    recv[place] = half[place]

    @pl.loop(0, rows, unroll=2)
    def _(r):
        standard, inverse = standardized(own_ref[r])
        scaled = dot(mixer, gp[r], TN) * scale
        first = jnp.mean(scaled, axis=0, keepdims=True)
        second = jnp.mean(scaled * standard, axis=0, keepdims=True)
        out_ref[r] = (
            cot_ref[r].astype(F32) + (scaled - first - standard * second) * inverse
        ).astype(BF16)

    wait_bytes(recv.at[others], main_rs.at[1])

    def add(i, total):
        return total + recv[i].astype(F32)

    total = lax.fori_loop(0, groups, add, jnp.zeros(recv.shape[1:], F32))
    gath[core, place] = rounded(total)

    @pl.loop(1, groups)
    def _(d):
        p = lax.rem(place + d, groups)
        remote(
            gath.at[core, place], gath.at[core, place], main_ag, device(2 * p + core)
        ).start()

    wait_bytes(half.at[others], main_ag.at[1])
    back = remote(gath.at[core], gath.at[core], pair_ag, partner)
    back.start()
    back.wait_recv()

    left = gath[0].reshape(groups * piece, 128).astype(F32)
    right = gath[1].reshape(groups * piece, 128).astype(F32)
    full = right + pltpu.roll(right, 96, 1)
    s = jnp.concatenate([left[0:n1], right[0:n1, 0:64]], axis=1)
    gsum = full[0:n1, 64:65]
    triple_ref[...] = s * scale_ref[...] + gsum * offset_ref[...]
    stencil_out_ref[...] = full[0:n1, 72:81]
    outgoing_ref[...] = jnp.concatenate([left[n1:n2], right[n1:n2, 0:64]], axis=1)
    sharp_out_ref[...] = full[n1 : n1 + 1, 64:68]
    eye = lax.broadcasted_iota(jnp.int32, (channels, channels), 0) == lax.broadcasted_iota(
        jnp.int32, (channels, channels), 1
    )
    scaling_ref[...] = jnp.sum(jnp.where(eye, full[n1:n2, 72:73], 0.0), axis=0, keepdims=True)
    offset_out_ref[...] = jnp.sum(mixer_f * gsum, axis=0, keepdims=True)

    @pl.when(has_hi)
    def _():
        for copy in to_next():
            copy.wait_send()

    @pl.when(has_lo)
    def _():
        for copy in to_previous():
            copy.wait_send()

    @pl.when(owner)
    def _():
        wait_bytes(gram.at[pl.ds(0, owners - 1)], gram_rs.at[0])
        wait_bytes(gram_recv.at[rest], gram_ag.at[0])

    @pl.when(jnp.logical_not(owner))
    def _():
        wait_bytes(gram, gram_rs.at[0])

    swap.wait_send()
    wait_bytes(recv.at[others], main_rs.at[0])
    wait_bytes(half.at[others], main_ag.at[0])
    back.wait_send()


def local(
    block_feature_map, upstream_sensitivity, triple_mixer, spatial_stencil, outgoing_mixer,
    sharpness_factor, standardize_scaling, standardize_offset,
):
    _, channels, rows, width = block_feature_map.shape
    n_img = lax.axis_size("img")
    n_tile = lax.axis_size("tile")
    groups = n_img * n_tile // 2
    own = jnp.transpose(block_feature_map[0], (1, 0, 2))
    cot = jnp.transpose(upstream_sensitivity[0], (1, 0, 2))
    n1 = 3 * channels
    each = -(-channels // (n_tile * 8)) * 8
    owners = -(-channels // each)
    piece = -(-4 * channels // (groups * 16)) * 16

    shape = jax.ShapeDtypeStruct
    vmem = pltpu.VMEM
    pair_sem = pltpu.SemaphoreType.DMA((2,))
    out, triple, stencil, outgoing, sharp, scaling, offset = pl.pallas_call(
        functools.partial(kernel, n_img, n_tile),
        out_shape=(
            shape((rows, channels, width), BF16),
            shape((n1, channels), F32),
            shape((n1, 9), F32),
            shape((channels, channels), F32),
            shape((1, sharpness_factor.shape[0]), F32),
            shape((1, channels), F32),
            shape((1, channels), F32),
        ),
        in_specs=[VMEM] * 7 + [SMEM],
        out_specs=[VMEM] * 7,
        scratch_shapes=[
            vmem((3, channels, width), BF16),
            vmem((3, channels, width), BF16),
            vmem((rows + 4, n1, width), BF16),
            vmem((rows + 2, n1, width), BF16),
            vmem((rows + 2, channels, width), BF16),
            vmem((rows + 2, n1, width), BF16),
            vmem((rows, n1, width), BF16),
            vmem((5, channels, 256), F32),
            vmem((owners, each, 128), F32),
            vmem((n_tile, each, 128), F32),
            vmem((owners, each, 128), F32),
            vmem((channels, channels), BF16),
            vmem((channels, channels), BF16),
            vmem((channels, channels), BF16),
            vmem((channels, 128), F32),
            vmem((n1, 256), F32),
            vmem((4 * channels, 128), F32),
            vmem((2, groups, piece, 128), BF16),
            vmem((groups, piece, 128), BF16),
            vmem((groups, piece, 128), BF16),
            vmem((groups, piece, 128), BF16),
            vmem((2, groups, piece, 128), BF16),
        ]
        + [pair_sem] * 10,
        compiler_params=pltpu.CompilerParams(
            collective_id=0, has_side_effects=True, vmem_limit_bytes=LIMIT
        ),
        name="block",
    )(
        own, cot, triple_mixer, spatial_stencil.reshape(n1, 9), outgoing_mixer,
        standardize_scaling.reshape(1, channels), standardize_offset.reshape(1, channels),
        sharpness_factor,
    )
    return (
        jnp.transpose(out, (1, 0, 2))[None],
        triple,
        stencil.reshape(n1, 3, 3),
        outgoing,
        sharp[0],
        scaling[0],
        offset[0],
    )


def solution(mesh):
    rows = P("img", None, "tile", None)
    return jax.shard_map(
        local,
        mesh=mesh,
        in_specs=(rows, rows, P(), P(), P(), P(), P(), P()),
        out_specs=(rows, P(), P(), P(), P(), P(), P()),
        check_vma=False,
    )
```

```python
import functools
import jax
import jax.numpy as jnp
from jax import lax
from jax.experimental import pallas as pl
from jax.experimental.pallas import tpu as pltpu
from jax.sharding import PartitionSpec as P

F32 = jnp.float32
BF16 = jnp.bfloat16
NT = (((1,), (1,)), ((), ()))
NN = (((1,), (0,)), ((), ()))
TN = (((0,), (0,)), ((), ()))
VMEM = pl.BlockSpec(memory_space=pltpu.VMEM)
SMEM = pl.BlockSpec(memory_space=pltpu.SMEM)
LIMIT = 56 * 1024 * 1024


def dot(a, b, dims=NN):
    return lax.dot_general(a, b, dims, preferred_element_type=F32)


def standardized(x):
    xf = x.astype(F32)
    centered = xf - jnp.mean(xf, axis=0, keepdims=True)
    inverse = lax.rsqrt(jnp.mean(centered * centered, axis=0, keepdims=True) + 1e-05)
    return centered * inverse, inverse


def shifted(v, lanes):
    width = v.shape[-1]
    right = jnp.where(lanes == 0, 0.0, pltpu.roll(v, 1, 1))
    left = jnp.where(lanes == width - 1, 0.0, pltpu.roll(v, width - 1, 1))
    return right, left


def column(row):
    n = row.shape[1]
    eye = lax.broadcasted_iota(jnp.int32, (n, n), 0) == lax.broadcasted_iota(jnp.int32, (n, n), 1)
    return jnp.sum(jnp.where(eye, row, 0.0), axis=1, keepdims=True)


def remote(src, dst, sems, ids):
    return pltpu.make_async_remote_copy(
        src_ref=src, dst_ref=dst, send_sem=sems.at[0], recv_sem=sems.at[1], device_id=ids,
        device_id_type=pl.DeviceIdType.MESH,
    )


def wait_bytes(ref, sem):
    pltpu.make_async_copy(ref, ref, sem).wait()


def kernel(
    n_img, n_tile,
    own_in, cot_in, mixer_t, stencil_in, out_mixer_ref, scale_ref, offset_ref, sharp_ref,
    out_ref, triple_ref, stencil_out_ref, outgoing_ref, sharp_out_ref, scaling_ref, offset_out_ref,
    own32, cot32, own_ref, cot_ref, mixer_ref, om_t, stencil_ref, lo, hi, proj, mixed, ga, gm, gp, acc, gram, gram_recv, gram_all, gg_ref, ggt_ref, at_ref, coef,
    sacc, extra, red, pair, half, recv, gath,
    lo_x, lo_c, hi_x, hi_c, gram_rs, gram_ag, pair_rs, main_rs, pair_ag, ag_send, ag_recv,
):
    channels, rows, width = own_in.shape
    heads = channels // 48
    img = lax.axis_index("img")
    tile = lax.axis_index("tile")
    n = n_img * n_tile
    me = img * n_tile + tile

    def device(p):
        return {"img": lax.div(p, n_tile), "tile": lax.rem(p, n_tile)}

    barrier = pltpu.get_barrier_semaphore()

    @pl.loop(1, n)
    def _(d):
        pl.semaphore_signal(
            barrier, inc=1, device_id=device(lax.rem(me + d, n)),
            device_id_type=pl.DeviceIdType.MESH,
        )

    def line_of(ref, r):
        return jnp.concatenate(
            [ref[pl.ds(c * channels * rows + r, channels, stride=rows), :] for c in range(width // 128)],
            axis=1,
        )

    for c in range(width // 128):
        part = pl.ds(c * channels * rows, channels * rows)
        cols = slice(128 * c, 128 * c + 128)
        own32[part, :] = own_in[:, :, cols].astype(F32).reshape(channels * rows, 128)
        cot32[part, :] = cot_in[:, :, cols].astype(F32).reshape(channels * rows, 128)
    for r in range(rows):
        own_ref[r] = line_of(own32, r).astype(BF16)
        cot_ref[r] = line_of(cot32, r).astype(BF16)

    mixer_ref[...] = mixer_t[...].T
    om_t[...] = out_mixer_ref[...].T
    taps = jnp.concatenate(
        [stencil_in[t // 3, t % 3 : t % 3 + 1, :] for t in range(9)]
        + [jnp.zeros((119, 3 * channels), F32)], axis=0,
    )
    stencil_ref[...] = taps.T

    pl.semaphore_wait(barrier, n - 1)

    def to_next():
        ids = {"img": img, "tile": tile + 1}
        return (
            remote(own_ref.at[pl.ds(rows - 2, 2)], lo.at[pl.ds(0, 2)], lo_x, ids),
            remote(cot_ref.at[pl.ds(rows - 1, 1)], lo.at[pl.ds(2, 1)], lo_c, ids),
        )

    def to_previous():
        ids = {"img": img, "tile": tile - 1}
        return (
            remote(own_ref.at[pl.ds(0, 2)], hi.at[pl.ds(0, 2)], hi_x, ids),
            remote(cot_ref.at[pl.ds(0, 1)], hi.at[pl.ds(2, 1)], hi_c, ids),
        )

    has_lo = tile > 0
    has_hi = tile < n_tile - 1

    @pl.when(has_hi)
    def _():
        for copy in to_next():
            copy.start()

    @pl.when(has_lo)
    def _():
        for copy in to_previous():
            copy.start()

    scale = column(scale_ref[...])
    offset = column(offset_ref[...])

    def project(x):
        standard, _ = standardized(x)
        normed = (standard * scale + offset).astype(BF16)
        return dot(mixer_ref[...], normed).astype(BF16)

    @pl.loop(0, rows, unroll=2)
    def _(r):
        proj[r + 2] = project(own_ref[r])
        ga[r + 1] = dot(om_t[...], cot_ref[r]).astype(BF16)

    @pl.when(has_lo)
    def _():
        for copy in to_next():
            copy.wait_recv()
        for i in range(2):
            proj[i] = project(lo[i])
        ga[0] = dot(om_t[...], lo[2]).astype(BF16)

    @pl.when(jnp.logical_not(has_lo))
    def _():
        proj[0:2] = jnp.zeros((2,) + proj.shape[1:], BF16)
        ga[0] = jnp.zeros(ga.shape[1:], BF16)

    @pl.when(has_hi)
    def _():
        for copy in to_previous():
            copy.wait_recv()
        for i in range(2):
            proj[rows + 2 + i] = project(hi[i])
        ga[rows + 1] = dot(om_t[...], hi[2]).astype(BF16)

    @pl.when(jnp.logical_not(has_hi))
    def _():
        proj[rows + 2 : rows + 4] = jnp.zeros((2,) + proj.shape[1:], BF16)
        ga[rows + 1] = jnp.zeros(ga.shape[1:], BF16)

    group = 16
    lanes = lax.broadcasted_iota(jnp.int32, (group, width), 1)

    @pl.loop(0, 3 * channels // group)
    def _(g):
        at = pl.ds(pl.multiple_of(g * group, group), group)
        weights = stencil_ref[at, :]
        w = [jnp.broadcast_to(weights[:, t : t + 1], (group, width)) for t in range(9)]
        line = [proj[i, at, :].astype(F32) for i in range(2)]
        for r in range(rows + 2):
            line.append(proj[r + 2, at, :].astype(F32))
            sums = [
                w[b] * line[r] + w[3 + b] * line[r + 1] + w[6 + b] * line[r + 2] for b in range(3)
            ]
            right = jnp.where(lanes == 0, 0.0, pltpu.roll(sums[0], 1, 1))
            left = jnp.where(lanes == width - 1, 0.0, pltpu.roll(sums[2], width - 1, 1))
            mixed[r, at, :] = (sums[1] + right + left).astype(BF16)

    acc[...] = jnp.zeros_like(acc)

    @pl.loop(0, rows, unroll=2)
    def _(r):
        q = mixed[r + 1, 0:channels, :]
        k = mixed[r + 1, channels : 2 * channels, :]
        v = mixed[r + 1, 2 * channels : 3 * channels, :]
        acc[0, :, 0:channels] += dot(q, k, NT)
        acc[1, :, 0:channels] += dot(ga[r + 1], v, NT)
        acc[2, :, 0:channels] += dot(cot_ref[r], v, NT)
        qf = q.astype(F32)
        kf = k.astype(F32)
        acc[3] += qf * qf
        acc[4] += kf * kf

    each = gram.shape[1]
    owners = gram.shape[0]
    gram_rows = owners * each
    pieces = []
    for h in range(heads):
        a, b = 48 * h, 48 * (h + 1)
        qsq = jnp.sum(acc[3, a:b, :], axis=1, keepdims=True)
        ksq = jnp.sum(acc[4, a:b, :], axis=1, keepdims=True)
        pieces.append(
            jnp.concatenate(
                [acc[0, a:b, a:b], acc[1, a:b, a:b], qsq, ksq, jnp.zeros((48, 30), F32)], axis=1,
            )
        )
    if gram_rows > channels:
        pieces.append(jnp.zeros((gram_rows - channels, 128), F32))
    packed = jnp.concatenate(pieces, axis=0)
    for i in range(owners):
        gram[i] = packed[i * each : (i + 1) * each]

    owner = tile < owners
    rest = pl.ds(0, n_tile - 1)

    @pl.loop(1, n_tile)
    def _(d):
        p = lax.rem(tile + d, n_tile)

        @pl.when(p < owners)
        def _():
            remote(gram.at[p], gram_recv.at[tile], gram_rs, {"img": img, "tile": p}).start()

    @pl.when(owner)
    def _():
        gram_recv[tile] = gram[tile]
        wait_bytes(gram_recv.at[rest], gram_rs.at[1])

        def add_gram(i, total):
            return total + gram_recv[i]

        gram_all[tile] = lax.fori_loop(0, n_tile, add_gram, jnp.zeros(gram.shape[1:], F32))

        @pl.loop(1, n_tile)
        def _(d):
            p = lax.rem(tile + d, n_tile)
            remote(gram_all.at[tile], gram_all.at[tile], gram_ag, {"img": img, "tile": p}).start()

    gg_ref[...] = jnp.zeros_like(gg_ref)
    ggt_ref[...] = jnp.zeros_like(ggt_ref)
    at_ref[...] = jnp.zeros_like(at_ref)
    extra[...] = jnp.zeros_like(extra)
    sacc[...] = jnp.zeros_like(sacc)

    @pl.when(owner)
    def _():
        wait_bytes(gram_all.at[pl.ds(0, owners - 1)], gram_ag.at[1])

    @pl.when(jnp.logical_not(owner))
    def _():
        wait_bytes(gram_all, gram_ag.at[1])

    whole = jnp.concatenate([gram_all[i] for i in range(owners)], axis=0)

    eye = lax.broadcasted_iota(jnp.int32, (48, 48), 0) == lax.broadcasted_iota(
        jnp.int32, (48, 48), 1
    )
    lane = lax.broadcasted_iota(jnp.int32, (1, 128), 1)
    leading = (tile == 0).astype(F32)
    for h in range(heads):
        a, b = 48 * h, 48 * (h + 1)
        gram_raw = whole[a:b, 0:48]
        grad_att = whole[a:b, 48:96]
        qsq = whole[a:b, 96:97]
        ksq_col = whole[a:b, 97:98]
        ksq = jnp.sum(jnp.where(eye, ksq_col, 0.0), axis=0, keepdims=True)
        lengths = jnp.sqrt(qsq + 1e-06) * jnp.sqrt(ksq + 1e-06)
        cosine = gram_raw / lengths
        e = jnp.exp(cosine * sharp_ref[h])
        attention = e / jnp.sum(e, axis=1, keepdims=True)
        grad_scores = attention * (grad_att - jnp.sum(attention * grad_att, axis=1, keepdims=True))
        sharp_sum = leading * jnp.sum(
            jnp.sum(grad_scores * cosine, axis=1, keepdims=True), axis=0, keepdims=True
        )
        extra[3 * channels : 3 * channels + 1, :] += jnp.where(lane == 64 + h, sharp_sum, 0.0)
        grad_cos = grad_scores * sharp_ref[h]
        gg = grad_cos / lengths
        terms = grad_cos * cosine
        gg_ref[a:b, a:b] = gg.astype(BF16)
        ggt_ref[a:b, a:b] = gg.T.astype(BF16)
        at_ref[a:b, a:b] = attention.T.astype(BF16)
        coef[a:b, 0:1] = jnp.sum(terms, axis=1, keepdims=True) / (qsq + 1e-06)
        kc = jnp.sum(terms, axis=0, keepdims=True) / (ksq + 1e-06)
        coef[a:b, 1:2] = jnp.sum(jnp.where(eye, kc, 0.0), axis=1, keepdims=True)

    oma = dot(acc[2, :, 0:channels].astype(BF16), at_ref[...])

    qc = coef[:, 0:1]
    kc = coef[:, 1:2]

    @pl.loop(0, rows + 2, unroll=2)
    def _(r):
        inside = jnp.logical_and(
            jnp.logical_or(r > 0, has_lo), jnp.logical_or(r < rows + 1, has_hi)
        ).astype(F32)
        q = mixed[r, 0:channels, :]
        k = mixed[r, channels : 2 * channels, :]
        gq = dot(gg_ref[...], k) - q.astype(F32) * qc
        gk = dot(ggt_ref[...], q) - k.astype(F32) * kc
        gv = dot(at_ref[...], ga[r])
        gm[r, 0:channels, :] = (gq * inside).astype(BF16)
        gm[r, channels : 2 * channels, :] = (gk * inside).astype(BF16)
        gm[r, 2 * channels : 3 * channels, :] = (gv * inside).astype(BF16)

    lane_g = lax.broadcasted_iota(jnp.int32, (group, 128), 1)

    @pl.loop(0, 3 * channels // group)
    def _(g):
        at = pl.ds(pl.multiple_of(g * group, group), group)
        weights = stencil_ref[at, :]
        w = [jnp.broadcast_to(weights[:, t : t + 1], (group, width)) for t in range(9)]
        line = [gm[i, at, :].astype(F32) for i in range(2)]
        for r in range(rows):
            line.append(gm[r + 2, at, :].astype(F32))
            sums = [
                w[b] * line[r + 2] + w[3 + b] * line[r + 1] + w[6 + b] * line[r] for b in range(3)
            ]
            left = jnp.where(lanes == width - 1, 0.0, pltpu.roll(sums[0], width - 1, 1))
            right = jnp.where(lanes == 0, 0.0, pltpu.roll(sums[2], 1, 1))
            gp[r, at, :] = (sums[1] + right + left).astype(BF16)

    @pl.loop(0, 3 * channels // group)
    def _(g):
        at = pl.ds(pl.multiple_of(g * group, group), group)
        tap = [jnp.zeros((group, 128), F32) for _ in range(9)]
        line = [proj[1 + i, at, :].astype(F32) for i in range(2)]
        for r in range(rows):
            line.append(proj[r + 3, at, :].astype(F32))
            g_mid = gm[r + 1, at, :].astype(F32)
            right, left = shifted(g_mid, lanes)
            for a in range(3):
                for b, side in enumerate((left, g_mid, right)):
                    for c in range(0, width, 128):
                        tap[3 * a + b] += line[r + a][:, c : c + 128] * side[:, c : c + 128]
        total = jnp.zeros((group, 128), F32)
        for t in range(9):
            s = jnp.sum(tap[t], axis=1, keepdims=True)
            total = total + jnp.where(lane_g == 72 + t, s, 0.0)
        extra[at, :] = total

    @pl.loop(0, rows, unroll=2)
    def _(r):
        standard, _ = standardized(own_ref[r])
        ext = jnp.concatenate([standard.astype(BF16), jnp.ones((64, width), BF16)], axis=0)
        sacc[...] += dot(gp[r], ext, NT)

    n1 = 3 * channels
    n2 = 4 * channels
    groups, piece = half.shape[:2]
    tail = sacc[:, 128:256]
    tail_lane = lax.broadcasted_iota(jnp.int32, tail.shape, 1)
    tail = jnp.where(tail_lane <= 64, tail, 0.0)
    mixer_f = mixer_ref[...].astype(F32)
    scaling_part = jnp.sum(mixer_f * sacc[:, 0:channels], axis=0, keepdims=True)
    oma_lane = lax.broadcasted_iota(jnp.int32, (channels, 128), 1)
    oma_tail = jnp.concatenate([oma[:, 128:192], jnp.zeros((channels, 64), F32)], axis=1)
    oma_tail = oma_tail + jnp.where(oma_lane == 72, column(scaling_part), 0.0)

    def split_again(x):
        at = lax.broadcasted_iota(jnp.int32, x.shape, x.ndim - 1)
        both = x + pltpu.roll(x, 96, x.ndim - 1)
        high = both.astype(BF16).astype(F32)
        low = pltpu.roll(both - high, 32, x.ndim - 1)
        return jnp.where(at < 64, x, jnp.where(at < 96, high, low))

    spare = groups * piece - n2
    filler = [jnp.zeros((spare, 128), BF16)] if spare else []
    head_part = [sacc[:, 0:128].astype(BF16), oma[:, 0:128].astype(BF16)] + filler
    tail_part = [
        split_again(tail + extra[0:n1, :]).astype(BF16),
        split_again(oma_tail + extra[n1:, :]).astype(BF16),
    ] + filler
    red[0] = jnp.concatenate(head_part, axis=0).reshape(half.shape)
    red[1] = jnp.concatenate(tail_part, axis=0).reshape(half.shape)

    core = lax.rem(tile, 2)
    place = lax.div(me, 2)
    partner = {"img": img, "tile": tile + 1 - 2 * core}
    others = pl.ds(0, groups - 1)

    def feature_rows(first_row, last_row):
        @pl.loop(first_row, last_row, unroll=2)
        def _(r):
            standard, inverse = standardized(own_ref[r])
            scaled = dot(mixer_t[...], gp[r]) * scale
            first = jnp.mean(scaled, axis=0, keepdims=True)
            second = jnp.mean(scaled * standard, axis=0, keepdims=True)
            adjoint = cot_ref[r].astype(F32) + (scaled - first - standard * second) * inverse
            for c in range(width // 128):
                own32[pl.ds(c * channels * rows + r, channels, stride=rows), :] = adjoint[
                    :, 128 * c : 128 * c + 128
                ]

    swap = remote(red.at[1 - core], pair, pair_rs, partner)
    swap.start()
    feature_rows(0, 2)
    swap.wait_recv()

    def rounded(x):
        return jnp.where(core == 1, split_again(x), x).astype(BF16)

    def add_pair(i, _):
        half[i] = rounded(red[core, i].astype(F32) + pair[i].astype(F32))
        return 0

    lax.fori_loop(0, groups, add_pair, 0)

    @pl.loop(1, groups)
    def _(d):
        p = lax.rem(place + d, groups)
        remote(half.at[p], recv.at[place], main_rs, device(2 * p + core)).start()

    recv[place] = half[place]

    feature_rows(2, rows)
    for c in range(width // 128):
        part = own32[pl.ds(c * channels * rows, channels * rows), :]
        out_ref[:, :, 128 * c : 128 * c + 128] = part.reshape(channels, rows, 128).astype(BF16)
    wait_bytes(recv.at[others], main_rs.at[1])

    def add(i, total):
        return total + recv[i].astype(F32)

    total = lax.fori_loop(0, groups, add, jnp.zeros(recv.shape[1:], F32))
    gath[core, place] = rounded(total)

    @pl.loop(1, groups)
    def _(d):
        p = lax.rem(place + d, groups)
        pltpu.make_async_remote_copy(
            src_ref=gath.at[core, place], dst_ref=gath.at[core, place], send_sem=ag_send,
            recv_sem=ag_recv.at[place], device_id=device(2 * p + core),
            device_id_type=pl.DeviceIdType.MESH,
        ).start()

    remote(gath.at[core, place], gath.at[core, place], pair_ag, partner).start()

    @pl.loop(1, groups)
    def _(d):
        p = lax.rem(place + groups - d, groups)
        wait_bytes(gath.at[core, p], ag_recv.at[p])
        remote(gath.at[core, p], gath.at[core, p], pair_ag, partner).start()

    wait_bytes(gath.at[1 - core], pair_ag.at[1])

    left = gath[0].reshape(groups * piece, 128).astype(F32)
    right = gath[1].reshape(groups * piece, 128).astype(F32)
    full = right + pltpu.roll(right, 96, 1)
    s = jnp.concatenate([left[0:n1], right[0:n1, 0:64]], axis=1)
    gsum = full[0:n1, 64:65]
    triple_ref[...] = s * scale_ref[...] + gsum * offset_ref[...]
    stencil_out_ref[...] = full[0:n1, 72:81]
    outgoing_ref[...] = jnp.concatenate([left[n1:n2], right[n1:n2, 0:64]], axis=1)
    sharp_out_ref[...] = full[n1 : n1 + 1, 64:68]
    eye = lax.broadcasted_iota(jnp.int32, (channels, channels), 0) == lax.broadcasted_iota(
        jnp.int32, (channels, channels), 1
    )
    scaling_ref[...] = jnp.sum(jnp.where(eye, full[n1:n2, 72:73], 0.0), axis=0, keepdims=True)
    offset_out_ref[...] = jnp.sum(mixer_f * gsum, axis=0, keepdims=True)

    @pl.when(has_hi)
    def _():
        for copy in to_next():
            copy.wait_send()

    @pl.when(has_lo)
    def _():
        for copy in to_previous():
            copy.wait_send()

    @pl.when(owner)
    def _():
        wait_bytes(gram.at[pl.ds(0, owners - 1)], gram_rs.at[0])
        wait_bytes(gram_recv.at[rest], gram_ag.at[0])

    @pl.when(jnp.logical_not(owner))
    def _():
        wait_bytes(gram, gram_rs.at[0])

    swap.wait_send()
    wait_bytes(recv.at[others], main_rs.at[0])
    wait_bytes(half.at[others], ag_send)
    wait_bytes(gath.at[core], pair_ag.at[0])


def local(
    block_feature_map, upstream_sensitivity, triple_mixer, spatial_stencil, outgoing_mixer,
    sharpness_factor, standardize_scaling, standardize_offset,
):
    _, channels, rows, width = block_feature_map.shape
    n_img = lax.axis_size("img")
    n_tile = lax.axis_size("tile")
    groups = n_img * n_tile // 2
    n1 = 3 * channels
    each = -(-channels // (n_tile * 8)) * 8
    owners = -(-channels // each)
    piece = -(-4 * channels // (groups * 16)) * 16

    shape = jax.ShapeDtypeStruct
    vmem = pltpu.VMEM
    pair_sem = pltpu.SemaphoreType.DMA((2,))
    out, triple, stencil, outgoing, sharp, scaling, offset = pl.pallas_call(
        functools.partial(kernel, n_img, n_tile),
        out_shape=(
            shape((channels, rows, width), BF16),
            shape((n1, channels), F32),
            shape((n1, 9), F32),
            shape((channels, channels), F32),
            shape((1, sharpness_factor.shape[0]), F32),
            shape((1, channels), F32),
            shape((1, channels), F32),
        ),
        in_specs=[VMEM] * 7 + [SMEM],
        out_specs=[VMEM] * 7,
        scratch_shapes=[
            vmem((channels * rows * width // 128, 128), F32),
            vmem((channels * rows * width // 128, 128), F32),
            vmem((rows, channels, width), BF16),
            vmem((rows, channels, width), BF16),
            vmem((n1, channels), BF16),
            vmem((channels, channels), BF16),
            vmem((n1, 128), F32),
            vmem((3, channels, width), BF16),
            vmem((3, channels, width), BF16),
            vmem((rows + 4, n1, width), BF16),
            vmem((rows + 2, n1, width), BF16),
            vmem((rows + 2, channels, width), BF16),
            vmem((rows + 2, n1, width), BF16),
            vmem((rows, n1, width), BF16),
            vmem((5, channels, 256), F32),
            vmem((owners, each, 128), F32),
            vmem((n_tile, each, 128), F32),
            vmem((owners, each, 128), F32),
            vmem((channels, channels), BF16),
            vmem((channels, channels), BF16),
            vmem((channels, channels), BF16),
            vmem((channels, 128), F32),
            vmem((n1, 256), F32),
            vmem((4 * channels, 128), F32),
            vmem((2, groups, piece, 128), BF16),
            vmem((groups, piece, 128), BF16),
            vmem((groups, piece, 128), BF16),
            vmem((groups, piece, 128), BF16),
            vmem((2, groups, piece, 128), BF16),
        ]
        + [pair_sem] * 9
        + [pltpu.SemaphoreType.DMA, pltpu.SemaphoreType.DMA((groups,))],
        compiler_params=pltpu.CompilerParams(
            collective_id=0, has_side_effects=True, vmem_limit_bytes=LIMIT
        ),
        name="block",
    )(
        block_feature_map[0], upstream_sensitivity[0], triple_mixer.T,
        jnp.transpose(spatial_stencil, (1, 2, 0)), outgoing_mixer,
        standardize_scaling.reshape(1, channels), standardize_offset.reshape(1, channels),
        sharpness_factor,
    )
    return (
        out[None],
        triple,
        stencil.reshape(n1, 3, 3),
        outgoing,
        sharp[0],
        scaling[0],
        offset[0],
    )


def solution(mesh):
    rows = P("img", None, "tile", None)
    return jax.shard_map(
        local,
        mesh=mesh,
        in_specs=(rows, rows, P(), P(), P(), P(), P(), P()),
        out_specs=(rows, P(), P(), P(), P(), P(), P()),
        check_vma=False,
    )
```

```python
import functools
import jax
import jax.numpy as jnp
from jax import lax
from jax.experimental import pallas as pl
from jax.experimental.pallas import tpu as pltpu
from jax.sharding import PartitionSpec as P

F32 = jnp.float32
BF16 = jnp.bfloat16
NT = (((1,), (1,)), ((), ()))
NN = (((1,), (0,)), ((), ()))
TN = (((0,), (0,)), ((), ()))
VMEM = pl.BlockSpec(memory_space=pltpu.VMEM)
SMEM = pl.BlockSpec(memory_space=pltpu.SMEM)
LIMIT = 56 * 1024 * 1024


def dot(a, b, dims=NN):
    return lax.dot_general(a, b, dims, preferred_element_type=F32)


def standardized(x):
    xf = x.astype(F32)
    centered = xf - jnp.mean(xf, axis=0, keepdims=True)
    inverse = lax.rsqrt(jnp.mean(centered * centered, axis=0, keepdims=True) + 1e-05)
    return centered * inverse, inverse


def shifted(v, lanes):
    width = v.shape[-1]
    right = jnp.where(lanes == 0, 0.0, pltpu.roll(v, 1, 1))
    left = jnp.where(lanes == width - 1, 0.0, pltpu.roll(v, width - 1, 1))
    return right, left


def column(row):
    n = row.shape[1]
    eye = lax.broadcasted_iota(jnp.int32, (n, n), 0) == lax.broadcasted_iota(jnp.int32, (n, n), 1)
    return jnp.sum(jnp.where(eye, row, 0.0), axis=1, keepdims=True)


def remote(src, dst, sems, ids):
    return pltpu.make_async_remote_copy(
        src_ref=src, dst_ref=dst, send_sem=sems.at[0], recv_sem=sems.at[1], device_id=ids,
        device_id_type=pl.DeviceIdType.MESH,
    )


def wait_bytes(ref, sem):
    pltpu.make_async_copy(ref, ref, sem).wait()


def kernel(
    n_img, n_tile,
    own_in, cot_in, mixer_t, stencil_in, out_mixer_ref, scale_ref, offset_ref, sharp_ref,
    out_ref, gath_out,
    own32, cot32, std32, ext, inv, own_ref, cot_ref, mixer_ref, om_t, stencil_ref, lo, hi, proj, mixed, ga, gm, gp, acc, gram, gram_recv, gram_all, gg_ref, ggt_ref, at_ref, coef,
    sacc, extra, red, pair, half, recv, gath,
    lo_x, lo_c, hi_x, hi_c, gram_rs, gram_ag, pair_rs, main_rs, pair_ag, ag_send, ag_recv,
):
    channels, rows, width = own_in.shape
    heads = channels // 48
    img = lax.axis_index("img")
    tile = lax.axis_index("tile")
    n = n_img * n_tile
    me = img * n_tile + tile

    def device(p):
        return {"img": lax.div(p, n_tile), "tile": lax.rem(p, n_tile)}

    barrier = pltpu.get_barrier_semaphore()

    @pl.loop(1, n)
    def _(d):
        pl.semaphore_signal(
            barrier, inc=1, device_id=device(lax.rem(me + d, n)),
            device_id_type=pl.DeviceIdType.MESH,
        )

    def line_of(ref, r):
        return jnp.concatenate(
            [ref[pl.ds(c * channels * rows + r, channels, stride=rows), :] for c in range(width // 128)],
            axis=1,
        )

    for c in range(width // 128):
        part = pl.ds(c * channels * rows, channels * rows)
        cols = slice(128 * c, 128 * c + 128)
        own32[part, :] = own_in[:, :, cols].astype(F32).reshape(channels * rows, 128)
        cot32[part, :] = cot_in[:, :, cols].astype(F32).reshape(channels * rows, 128)
    for r in range(rows):
        own_ref[r] = line_of(own32, r).astype(BF16)
        cot_ref[r] = line_of(cot32, r).astype(BF16)

    mixer_ref[...] = mixer_t[...].T
    om_t[...] = out_mixer_ref[...].T
    taps = jnp.concatenate(
        [stencil_in[t // 3, t % 3 : t % 3 + 1, :] for t in range(9)]
        + [jnp.zeros((119, 3 * channels), F32)], axis=0,
    )
    stencil_ref[...] = taps.T

    pl.semaphore_wait(barrier, n - 1)

    def to_next():
        ids = {"img": img, "tile": tile + 1}
        return (
            remote(own_ref.at[pl.ds(rows - 2, 2)], lo.at[pl.ds(0, 2)], lo_x, ids),
            remote(cot_ref.at[pl.ds(rows - 1, 1)], lo.at[pl.ds(2, 1)], lo_c, ids),
        )

    def to_previous():
        ids = {"img": img, "tile": tile - 1}
        return (
            remote(own_ref.at[pl.ds(0, 2)], hi.at[pl.ds(0, 2)], hi_x, ids),
            remote(cot_ref.at[pl.ds(0, 1)], hi.at[pl.ds(2, 1)], hi_c, ids),
        )

    has_lo = tile > 0
    has_hi = tile < n_tile - 1

    @pl.when(has_hi)
    def _():
        for copy in to_next():
            copy.start()

    @pl.when(has_lo)
    def _():
        for copy in to_previous():
            copy.start()

    scale = column(scale_ref[...])
    offset = column(offset_ref[...])

    def project(x):
        standard, _ = standardized(x)
        normed = (standard * scale + offset).astype(BF16)
        return dot(mixer_ref[...], normed).astype(BF16)

    @pl.loop(0, rows, unroll=2)
    def _(r):
        standard, inverse = standardized(own_ref[r])
        std32[r] = standard
        inv[r] = inverse
        ext[r, 0:channels, :] = standard.astype(BF16)
        ext[r, channels:256, :] = jnp.ones((256 - channels, width), BF16)
        normed = (standard * scale + offset).astype(BF16)
        proj[r + 2] = dot(mixer_ref[...], normed).astype(BF16)
        ga[r + 1] = dot(om_t[...], cot_ref[r]).astype(BF16)

    @pl.when(has_lo)
    def _():
        to_next()[0].wait_recv()
        proj[1] = project(lo[1])

    @pl.when(jnp.logical_not(has_lo))
    def _():
        proj[0:2] = jnp.zeros((2,) + proj.shape[1:], BF16)
        ga[0] = jnp.zeros(ga.shape[1:], BF16)

    @pl.when(has_hi)
    def _():
        to_previous()[0].wait_recv()
        proj[rows + 2] = project(hi[0])

    @pl.when(jnp.logical_not(has_hi))
    def _():
        proj[rows + 2 : rows + 4] = jnp.zeros((2,) + proj.shape[1:], BF16)
        ga[rows + 1] = jnp.zeros(ga.shape[1:], BF16)

    group = 16
    lanes = lax.broadcasted_iota(jnp.int32, (group, width), 1)

    def mix(strips):
        @pl.loop(0, 3 * channels // group)
        def _(g):
            at = pl.ds(pl.multiple_of(g * group, group), group)
            weights = stencil_ref[at, :]
            w = [jnp.broadcast_to(weights[:, t : t + 1], (group, width)) for t in range(9)]
            for first_row, last_row in strips:
                line = [proj[first_row + i, at, :].astype(F32) for i in range(2)]
                for r in range(first_row, last_row):
                    line = line[-2:] + [proj[r + 2, at, :].astype(F32)]
                    sums = [w[b] * line[0] + w[3 + b] * line[1] + w[6 + b] * line[2] for b in range(3)]
                    right = jnp.where(lanes == 0, 0.0, pltpu.roll(sums[0], 1, 1))
                    left = jnp.where(lanes == width - 1, 0.0, pltpu.roll(sums[2], width - 1, 1))
                    mixed[r, at, :] = (sums[1] + right + left).astype(BF16)

    mix([(1, rows + 1)])

    acc[...] = jnp.zeros_like(acc)

    @pl.loop(0, rows, unroll=2)
    def _(r):
        q = mixed[r + 1, 0:channels, :]
        k = mixed[r + 1, channels : 2 * channels, :]
        v = mixed[r + 1, 2 * channels : 3 * channels, :]
        acc[0, :, 0:channels] += dot(q, k, NT)
        acc[1, :, 0:channels] += dot(ga[r + 1], v, NT)
        qf = q.astype(F32)
        kf = k.astype(F32)
        acc[3] += qf * qf
        acc[4] += kf * kf

    each = gram.shape[1]
    owners = gram.shape[0]
    gram_rows = owners * each
    pieces = []
    for h in range(heads):
        a, b = 48 * h, 48 * (h + 1)
        qsq = jnp.sum(acc[3, a:b, :], axis=1, keepdims=True)
        ksq = jnp.sum(acc[4, a:b, :], axis=1, keepdims=True)
        pieces.append(
            jnp.concatenate(
                [acc[0, a:b, a:b], acc[1, a:b, a:b], qsq, ksq, jnp.zeros((48, 30), F32)], axis=1,
            )
        )
    if gram_rows > channels:
        pieces.append(jnp.zeros((gram_rows - channels, 128), F32))
    packed = jnp.concatenate(pieces, axis=0)
    for i in range(owners):
        gram[i] = packed[i * each : (i + 1) * each]

    owner = tile < owners
    rest = pl.ds(0, n_tile - 1)

    @pl.loop(1, n_tile)
    def _(d):
        p = lax.rem(tile + d, n_tile)

        @pl.when(p < owners)
        def _():
            remote(gram.at[p], gram_recv.at[tile], gram_rs, {"img": img, "tile": p}).start()

    @pl.when(has_lo)
    def _():
        to_next()[1].wait_recv()
        proj[0] = project(lo[0])
        ga[0] = dot(om_t[...], lo[2]).astype(BF16)

    @pl.when(has_hi)
    def _():
        to_previous()[1].wait_recv()
        proj[rows + 3] = project(hi[1])
        ga[rows + 1] = dot(om_t[...], hi[2]).astype(BF16)

    mix([(0, 1), (rows + 1, rows + 2)])

    @pl.when(owner)
    def _():
        gram_recv[tile] = gram[tile]
        wait_bytes(gram_recv.at[rest], gram_rs.at[1])

        def add_gram(i, total):
            return total + gram_recv[i]

        gram_all[tile] = lax.fori_loop(0, n_tile, add_gram, jnp.zeros(gram.shape[1:], F32))

        @pl.loop(1, n_tile)
        def _(d):
            p = lax.rem(tile + d, n_tile)
            remote(gram_all.at[tile], gram_all.at[tile], gram_ag, {"img": img, "tile": p}).start()

    gg_ref[...] = jnp.zeros_like(gg_ref)
    ggt_ref[...] = jnp.zeros_like(ggt_ref)
    at_ref[...] = jnp.zeros_like(at_ref)
    extra[...] = jnp.zeros_like(extra)
    sacc[...] = jnp.zeros_like(sacc)

    @pl.loop(0, rows, unroll=2)
    def _(r):
        acc[2, :, 0:channels] += dot(cot_ref[r], mixed[r + 1, 2 * channels : 3 * channels, :], NT)


    @pl.when(owner)
    def _():
        wait_bytes(gram_all.at[pl.ds(0, owners - 1)], gram_ag.at[1])

    @pl.when(jnp.logical_not(owner))
    def _():
        wait_bytes(gram_all, gram_ag.at[1])

    whole = jnp.concatenate([gram_all[i] for i in range(owners)], axis=0)

    eye = lax.broadcasted_iota(jnp.int32, (48, 48), 0) == lax.broadcasted_iota(
        jnp.int32, (48, 48), 1
    )
    lane = lax.broadcasted_iota(jnp.int32, (1, 128), 1)
    leading = (tile == 0).astype(F32)
    for h in range(heads):
        a, b = 48 * h, 48 * (h + 1)
        gram_raw = whole[a:b, 0:48]
        grad_att = whole[a:b, 48:96]
        qsq = whole[a:b, 96:97]
        ksq_col = whole[a:b, 97:98]
        ksq = jnp.sum(jnp.where(eye, ksq_col, 0.0), axis=0, keepdims=True)
        lengths = jnp.sqrt(qsq + 1e-06) * jnp.sqrt(ksq + 1e-06)
        cosine = gram_raw / lengths
        e = jnp.exp(cosine * sharp_ref[h])
        attention = e / jnp.sum(e, axis=1, keepdims=True)
        grad_scores = attention * (grad_att - jnp.sum(attention * grad_att, axis=1, keepdims=True))
        sharp_sum = leading * jnp.sum(
            jnp.sum(grad_scores * cosine, axis=1, keepdims=True), axis=0, keepdims=True
        )
        extra[3 * channels : 3 * channels + 1, :] += jnp.where(lane == 64 + h, sharp_sum, 0.0)
        grad_cos = grad_scores * sharp_ref[h]
        gg = grad_cos / lengths
        terms = grad_cos * cosine
        gg_ref[a:b, a:b] = gg.astype(BF16)
        ggt_ref[a:b, a:b] = gg.T.astype(BF16)
        at_ref[a:b, a:b] = attention.T.astype(BF16)
        coef[a:b, 0:1] = jnp.sum(terms, axis=1, keepdims=True) / (qsq + 1e-06)
        kc = jnp.sum(terms, axis=0, keepdims=True) / (ksq + 1e-06)
        coef[a:b, 1:2] = jnp.sum(jnp.where(eye, kc, 0.0), axis=1, keepdims=True)

    oma = dot(acc[2, :, 0:channels].astype(BF16), at_ref[...])

    qc = coef[:, 0:1]
    kc = coef[:, 1:2]

    @pl.loop(0, rows + 2, unroll=2)
    def _(r):
        inside = jnp.logical_and(
            jnp.logical_or(r > 0, has_lo), jnp.logical_or(r < rows + 1, has_hi)
        ).astype(F32)
        q = mixed[r, 0:channels, :]
        k = mixed[r, channels : 2 * channels, :]
        gq = dot(gg_ref[...], k) - q.astype(F32) * qc
        gk = dot(ggt_ref[...], q) - k.astype(F32) * kc
        gv = dot(at_ref[...], ga[r])
        gm[r, 0:channels, :] = (gq * inside).astype(BF16)
        gm[r, channels : 2 * channels, :] = (gk * inside).astype(BF16)
        gm[r, 2 * channels : 3 * channels, :] = (gv * inside).astype(BF16)

    lane_g = lax.broadcasted_iota(jnp.int32, (group, 128), 1)

    @pl.loop(0, 3 * channels // group)
    def _(g):
        at = pl.ds(pl.multiple_of(g * group, group), group)
        weights = stencil_ref[at, :]
        w = [jnp.broadcast_to(weights[:, t : t + 1], (group, width)) for t in range(9)]
        line = [gm[i, at, :].astype(F32) for i in range(2)]
        for r in range(rows):
            line.append(gm[r + 2, at, :].astype(F32))
            sums = [
                w[b] * line[r + 2] + w[3 + b] * line[r + 1] + w[6 + b] * line[r] for b in range(3)
            ]
            left = jnp.where(lanes == width - 1, 0.0, pltpu.roll(sums[0], width - 1, 1))
            right = jnp.where(lanes == 0, 0.0, pltpu.roll(sums[2], 1, 1))
            gp[r, at, :] = (sums[1] + right + left).astype(BF16)

    @pl.loop(0, 3 * channels // group)
    def _(g):
        at = pl.ds(pl.multiple_of(g * group, group), group)
        tap = [jnp.zeros((group, 128), F32) for _ in range(9)]
        line = [proj[1 + i, at, :].astype(F32) for i in range(2)]
        for r in range(rows):
            line.append(proj[r + 3, at, :].astype(F32))
            g_mid = gm[r + 1, at, :].astype(F32)
            right, left = shifted(g_mid, lanes)
            for a in range(3):
                for b, side in enumerate((left, g_mid, right)):
                    for c in range(0, width, 128):
                        tap[3 * a + b] += line[r + a][:, c : c + 128] * side[:, c : c + 128]
        total = jnp.zeros((group, 128), F32)
        for t in range(9):
            s = jnp.sum(tap[t], axis=1, keepdims=True)
            total = total + jnp.where(lane_g == 72 + t, s, 0.0)
        extra[at, :] = total

    @pl.loop(0, rows, unroll=2)
    def _(r):
        sacc[...] += dot(gp[r], ext[r], NT)

    n1 = 3 * channels
    n2 = 4 * channels
    groups, piece = half.shape[:2]
    tail = sacc[:, 128:256]
    tail_lane = lax.broadcasted_iota(jnp.int32, tail.shape, 1)
    tail = jnp.where(tail_lane <= 64, tail, 0.0)
    mixer_f = mixer_ref[...].astype(F32)
    scaling_part = jnp.sum(mixer_f * sacc[:, 0:channels], axis=0, keepdims=True)
    oma_lane = lax.broadcasted_iota(jnp.int32, (channels, 128), 1)
    oma_tail = jnp.concatenate([oma[:, 128:192], jnp.zeros((channels, 64), F32)], axis=1)
    oma_tail = oma_tail + jnp.where(oma_lane == 72, column(scaling_part), 0.0)

    def split_again(x):
        at = lax.broadcasted_iota(jnp.int32, x.shape, x.ndim - 1)
        both = x + pltpu.roll(x, 96, x.ndim - 1)
        high = both.astype(BF16).astype(F32)
        low = pltpu.roll(both - high, 32, x.ndim - 1)
        return jnp.where(at < 64, x, jnp.where(at < 96, high, low))

    spare = groups * piece - n2
    filler = [jnp.zeros((spare, 128), BF16)] if spare else []
    head_part = [sacc[:, 0:128].astype(BF16), oma[:, 0:128].astype(BF16)] + filler
    tail_part = [
        split_again(tail + extra[0:n1, :]).astype(BF16),
        split_again(oma_tail + extra[n1:, :]).astype(BF16),
    ] + filler
    red[0] = jnp.concatenate(head_part, axis=0).reshape(half.shape)
    red[1] = jnp.concatenate(tail_part, axis=0).reshape(half.shape)

    core = lax.rem(tile, 2)
    place = lax.div(me, 2)
    partner = {"img": img, "tile": tile + 1 - 2 * core}
    others = pl.ds(0, groups - 1)

    def feature_rows(first_row, last_row):
        @pl.loop(first_row, last_row, unroll=2)
        def _(r):
            standard = std32[r]
            inverse = inv[r]
            scaled = dot(mixer_t[...], gp[r]) * scale
            first = jnp.mean(scaled, axis=0, keepdims=True)
            second = jnp.mean(scaled * standard, axis=0, keepdims=True)
            adjoint = cot_ref[r].astype(F32) + (scaled - first - standard * second) * inverse
            for c in range(width // 128):
                own32[pl.ds(c * channels * rows + r, channels, stride=rows), :] = adjoint[
                    :, 128 * c : 128 * c + 128
                ]

    swap = remote(red.at[1 - core], pair, pair_rs, partner)
    swap.start()
    feature_rows(0, 2)
    swap.wait_recv()

    def rounded(x):
        return jnp.where(core == 1, split_again(x), x).astype(BF16)

    def add_pair(i, _):
        half[i] = rounded(red[core, i].astype(F32) + pair[i].astype(F32))
        return 0

    lax.fori_loop(0, groups, add_pair, 0)

    @pl.loop(1, groups)
    def _(d):
        p = lax.rem(place + d, groups)
        remote(half.at[p], recv.at[place], main_rs, device(2 * p + core)).start()

    recv[place] = half[place]

    feature_rows(2, 6)
    wait_bytes(recv.at[others], main_rs.at[1])

    def add(i, total):
        return total + recv[i].astype(F32)

    total = lax.fori_loop(0, groups, add, jnp.zeros(recv.shape[1:], F32))
    gath[core, place] = rounded(total)

    @pl.loop(1, groups)
    def _(d):
        p = lax.rem(place + d, groups)
        pltpu.make_async_remote_copy(
            src_ref=gath.at[core, place], dst_ref=gath.at[core, place], send_sem=ag_send,
            recv_sem=ag_recv.at[place], device_id=device(2 * p + core),
            device_id_type=pl.DeviceIdType.MESH,
        ).start()

    remote(gath.at[core, place], gath.at[core, place], pair_ag, partner).start()
    feature_rows(6, rows)
    for c in range(width // 128):
        part = own32[pl.ds(c * channels * rows, channels * rows), :]
        out_ref[:, :, 128 * c : 128 * c + 128] = part.reshape(channels, rows, 128).astype(BF16)

    @pl.loop(1, groups)
    def _(d):
        p = lax.rem(place + groups - d, groups)
        wait_bytes(gath.at[core, p], ag_recv.at[p])
        remote(gath.at[core, p], gath.at[core, p], pair_ag, partner).start()

    wait_bytes(gath.at[1 - core], pair_ag.at[1])

    gath_out[...] = gath[...]

    @pl.when(has_hi)
    def _():
        for copy in to_next():
            copy.wait_send()

    @pl.when(has_lo)
    def _():
        for copy in to_previous():
            copy.wait_send()

    @pl.when(owner)
    def _():
        wait_bytes(gram.at[pl.ds(0, owners - 1)], gram_rs.at[0])
        wait_bytes(gram_recv.at[rest], gram_ag.at[0])

    @pl.when(jnp.logical_not(owner))
    def _():
        wait_bytes(gram, gram_rs.at[0])

    swap.wait_send()
    wait_bytes(recv.at[others], main_rs.at[0])
    wait_bytes(half.at[others], ag_send)
    wait_bytes(gath.at[core], pair_ag.at[0])


def finish_kernel(
    adjoint_ref, gath_ref, mixer_t, scale_ref, offset_ref,
    out_ref, triple_ref, stencil_ref, outgoing_ref, sharp_ref, scaling_ref, offset_out_ref, sem,
):
    move = pltpu.make_async_copy(adjoint_ref, out_ref, sem)
    move.start()
    channels, n1 = mixer_t.shape
    n2 = n1 + channels
    left = gath_ref[0].reshape(-1, 128).astype(F32)
    right = gath_ref[1].reshape(-1, 128).astype(F32)
    full = right + pltpu.roll(right, 96, 1)
    s = jnp.concatenate([left[0:n1], right[0:n1, 0:64]], axis=1)
    gsum = full[0:n1, 64:65]
    triple_ref[...] = (s * scale_ref[...] + gsum * offset_ref[...]).T
    turned = full[0:n1].T
    for t in range(9):
        stencil_ref[t // 3, t % 3 : t % 3 + 1, :] = turned[72 + t : 73 + t, :]
    outgoing_ref[...] = jnp.concatenate([left[n1:n2], right[n1:n2, 0:64]], axis=1)
    sharp_ref[...] = full[n1 : n1 + 1, 64:68]
    scaling_ref[...] = full[n1:n2].T[72:73, :]
    mixer = mixer_t[...].T.astype(F32)
    offset_out_ref[...] = jnp.sum(mixer * gsum, axis=0, keepdims=True)
    move.wait()


def local(
    block_feature_map, upstream_sensitivity, triple_mixer, spatial_stencil, outgoing_mixer,
    sharpness_factor, standardize_scaling, standardize_offset,
):
    _, channels, rows, width = block_feature_map.shape
    n_img = lax.axis_size("img")
    n_tile = lax.axis_size("tile")
    groups = n_img * n_tile // 2
    n1 = 3 * channels
    each = -(-channels // (n_tile * 8)) * 8
    owners = -(-channels // each)
    piece = -(-4 * channels // (groups * 16)) * 16

    shape = jax.ShapeDtypeStruct
    vmem = pltpu.VMEM
    pair_sem = pltpu.SemaphoreType.DMA((2,))
    mixer_t = triple_mixer.T
    scale_row = standardize_scaling.reshape(1, channels)
    offset_row = standardize_offset.reshape(1, channels)
    adjoint, gathered = pl.pallas_call(
        functools.partial(kernel, n_img, n_tile),
        out_shape=(
            shape((channels, rows, width), BF16),
            shape((2, groups, piece, 128), BF16),
        ),
        in_specs=[VMEM] * 7 + [SMEM],
        out_specs=[VMEM] * 2,
        scratch_shapes=[
            vmem((channels * rows * width // 128, 128), F32),
            vmem((channels * rows * width // 128, 128), F32),
            vmem((rows, channels, width), F32),
            vmem((rows, 256, width), BF16),
            vmem((rows, 1, width), F32),
            vmem((rows, channels, width), BF16),
            vmem((rows, channels, width), BF16),
            vmem((n1, channels), BF16),
            vmem((channels, channels), BF16),
            vmem((n1, 128), F32),
            vmem((3, channels, width), BF16),
            vmem((3, channels, width), BF16),
            vmem((rows + 4, n1, width), BF16),
            vmem((rows + 2, n1, width), BF16),
            vmem((rows + 2, channels, width), BF16),
            vmem((rows + 2, n1, width), BF16),
            vmem((rows, n1, width), BF16),
            vmem((5, channels, 256), F32),
            vmem((owners, each, 128), F32),
            vmem((n_tile, each, 128), F32),
            vmem((owners, each, 128), F32),
            vmem((channels, channels), BF16),
            vmem((channels, channels), BF16),
            vmem((channels, channels), BF16),
            vmem((channels, 128), F32),
            vmem((n1, 256), F32),
            vmem((4 * channels, 128), F32),
            vmem((2, groups, piece, 128), BF16),
            vmem((groups, piece, 128), BF16),
            vmem((groups, piece, 128), BF16),
            vmem((groups, piece, 128), BF16),
            vmem((2, groups, piece, 128), BF16),
        ]
        + [pair_sem] * 9
        + [pltpu.SemaphoreType.DMA, pltpu.SemaphoreType.DMA((groups,))],
        compiler_params=pltpu.CompilerParams(
            collective_id=0, has_side_effects=True, vmem_limit_bytes=LIMIT
        ),
        name="block",
    )(
        block_feature_map[0], upstream_sensitivity[0], mixer_t,
        jnp.transpose(spatial_stencil, (1, 2, 0)), outgoing_mixer, scale_row, offset_row,
        sharpness_factor,
    )
    anywhere = pl.BlockSpec(memory_space=pl.ANY)
    out, triple, stencil, outgoing, sharp, scaling, offset = pl.pallas_call(
        finish_kernel,
        out_shape=(
            shape((channels, rows, width), BF16),
            shape((channels, n1), F32),
            shape((3, 3, n1), F32),
            shape((channels, channels), F32),
            shape((1, sharpness_factor.shape[0]), F32),
            shape((1, channels), F32),
            shape((1, channels), F32),
        ),
        in_specs=[anywhere] + [VMEM] * 4,
        out_specs=[anywhere] + [VMEM] * 6,
        scratch_shapes=[pltpu.SemaphoreType.DMA],
        compiler_params=pltpu.CompilerParams(vmem_limit_bytes=32 * 1024 * 1024),
        name="finish",
    )(adjoint, gathered, mixer_t, scale_row, offset_row)
    return (
        out[None],
        triple.T,
        jnp.transpose(stencil, (2, 0, 1)),
        outgoing,
        sharp[0],
        scaling[0],
        offset[0],
    )


def solution(mesh):
    rows = P("img", None, "tile", None)
    return jax.shard_map(
        local,
        mesh=mesh,
        in_specs=(rows, rows, P(), P(), P(), P(), P(), P()),
        out_specs=(rows, P(), P(), P(), P(), P(), P()),
        check_vma=False,
    )
```

```python
import functools
import jax
import jax.numpy as jnp
from jax import lax
from jax.experimental import pallas as pl
from jax.experimental.pallas import tpu as pltpu
from jax.sharding import PartitionSpec as P

F32 = jnp.float32
BF16 = jnp.bfloat16
NT = (((1,), (1,)), ((), ()))
NN = (((1,), (0,)), ((), ()))
TN = (((0,), (0,)), ((), ()))
VMEM = pl.BlockSpec(memory_space=pltpu.VMEM)
SMEM = pl.BlockSpec(memory_space=pltpu.SMEM)
LIMIT = 56 * 1024 * 1024


def dot(a, b, dims=NN):
    return lax.dot_general(a, b, dims, preferred_element_type=F32)


def standardized(x):
    xf = x.astype(F32)
    centered = xf - jnp.mean(xf, axis=0, keepdims=True)
    inverse = lax.rsqrt(jnp.mean(centered * centered, axis=0, keepdims=True) + 1e-05)
    return centered * inverse, inverse


def shifted(v, lanes):
    width = v.shape[-1]
    right = jnp.where(lanes == 0, 0.0, pltpu.roll(v, 1, 1))
    left = jnp.where(lanes == width - 1, 0.0, pltpu.roll(v, width - 1, 1))
    return right, left


def column(row):
    n = row.shape[1]
    eye = lax.broadcasted_iota(jnp.int32, (n, n), 0) == lax.broadcasted_iota(jnp.int32, (n, n), 1)
    return jnp.sum(jnp.where(eye, row, 0.0), axis=1, keepdims=True)


def remote(src, dst, sems, ids):
    return pltpu.make_async_remote_copy(
        src_ref=src, dst_ref=dst, send_sem=sems.at[0], recv_sem=sems.at[1], device_id=ids,
        device_id_type=pl.DeviceIdType.MESH,
    )


def wait_bytes(ref, sem):
    pltpu.make_async_copy(ref, ref, sem).wait()


def kernel(
    n_img, n_tile,
    own_in, cot_in, mixer_t, stencil_in, out_mixer_ref, scale_ref, offset_ref, sharp_ref,
    out_ref, gath_out,
    own32, cot32, std32, ext, inv, own_ref, cot_ref, mixer_ref, om_t, stencil_ref, lo, hi, proj, mixed, ga, gm, gp, acc, gram, gram_recv, gram_all, gg_ref, ggt_ref, at_ref, coef,
    sacc, extra, red, pair, half, recv, gath,
    lo_x, lo_c, hi_x, hi_c, gram_rs, gram_ag, pair_rs, main_rs, pair_ag, ag_send, ag_recv,
):
    channels, rows, width = own_in.shape
    heads = channels // 48
    img = lax.axis_index("img")
    tile = lax.axis_index("tile")
    n = n_img * n_tile
    me = img * n_tile + tile

    def device(p):
        return {"img": lax.div(p, n_tile), "tile": lax.rem(p, n_tile)}

    barrier = pltpu.get_barrier_semaphore()

    @pl.loop(1, n)
    def _(d):
        pl.semaphore_signal(
            barrier, inc=1, device_id=device(lax.rem(me + d, n)),
            device_id_type=pl.DeviceIdType.MESH,
        )

    def line_of(ref, r):
        return jnp.concatenate(
            [ref[pl.ds(c * channels * rows + r, channels, stride=rows), :] for c in range(width // 128)],
            axis=1,
        )

    for c in range(width // 128):
        part = pl.ds(c * channels * rows, channels * rows)
        cols = slice(128 * c, 128 * c + 128)
        own32[part, :] = own_in[:, :, cols].astype(F32).reshape(channels * rows, 128)
        cot32[part, :] = cot_in[:, :, cols].astype(F32).reshape(channels * rows, 128)
    for r in range(rows):
        own_ref[r] = line_of(own32, r).astype(BF16)
        cot_ref[r] = line_of(cot32, r).astype(BF16)

    mixer_ref[...] = mixer_t[...].T
    om_t[...] = out_mixer_ref[...].T
    taps = jnp.concatenate(
        [stencil_in[t // 3, t % 3 : t % 3 + 1, :] for t in range(9)]
        + [jnp.zeros((119, 3 * channels), F32)], axis=0,
    )
    stencil_ref[...] = taps.T

    pl.semaphore_wait(barrier, n - 1)

    def to_next():
        ids = {"img": img, "tile": tile + 1}
        return (
            remote(own_ref.at[pl.ds(rows - 2, 2)], lo.at[pl.ds(0, 2)], lo_x, ids),
            remote(cot_ref.at[pl.ds(rows - 1, 1)], lo.at[pl.ds(2, 1)], lo_c, ids),
        )

    def to_previous():
        ids = {"img": img, "tile": tile - 1}
        return (
            remote(own_ref.at[pl.ds(0, 2)], hi.at[pl.ds(0, 2)], hi_x, ids),
            remote(cot_ref.at[pl.ds(0, 1)], hi.at[pl.ds(2, 1)], hi_c, ids),
        )

    has_lo = tile > 0
    has_hi = tile < n_tile - 1

    @pl.when(has_hi)
    def _():
        for copy in to_next():
            copy.start()

    @pl.when(has_lo)
    def _():
        for copy in to_previous():
            copy.start()

    scale = column(scale_ref[...])
    offset = column(offset_ref[...])

    def project(x):
        standard, _ = standardized(x)
        normed = (standard * scale + offset).astype(BF16)
        return dot(mixer_ref[...], normed).astype(BF16)

    @pl.loop(0, rows, unroll=4)
    def _(r):
        standard, inverse = standardized(own_ref[r])
        std32[r] = standard
        inv[r] = inverse
        ext[r, 0:channels, :] = standard.astype(BF16)
        ext[r, channels:256, :] = jnp.ones((256 - channels, width), BF16)
        normed = (standard * scale + offset).astype(BF16)
        proj[r + 2] = dot(mixer_ref[...], normed).astype(BF16)
        ga[r + 1] = dot(om_t[...], cot_ref[r]).astype(BF16)

    @pl.when(has_lo)
    def _():
        to_next()[0].wait_recv()
        proj[1] = project(lo[1])

    @pl.when(jnp.logical_not(has_lo))
    def _():
        proj[0:2] = jnp.zeros((2,) + proj.shape[1:], BF16)
        ga[0] = jnp.zeros(ga.shape[1:], BF16)

    @pl.when(has_hi)
    def _():
        to_previous()[0].wait_recv()
        proj[rows + 2] = project(hi[0])

    @pl.when(jnp.logical_not(has_hi))
    def _():
        proj[rows + 2 : rows + 4] = jnp.zeros((2,) + proj.shape[1:], BF16)
        ga[rows + 1] = jnp.zeros(ga.shape[1:], BF16)

    group = 16
    lanes = lax.broadcasted_iota(jnp.int32, (group, width), 1)

    def mix(strips):
        @pl.loop(0, 3 * channels // group, unroll=2)
        def _(g):
            at = pl.ds(pl.multiple_of(g * group, group), group)
            weights = stencil_ref[at, :]
            w = [jnp.broadcast_to(weights[:, t : t + 1], (group, width)) for t in range(9)]
            for first_row, last_row in strips:
                line = [proj[first_row + i, at, :].astype(F32) for i in range(2)]
                for r in range(first_row, last_row):
                    line = line[-2:] + [proj[r + 2, at, :].astype(F32)]
                    sums = [w[b] * line[0] + w[3 + b] * line[1] + w[6 + b] * line[2] for b in range(3)]
                    right = jnp.where(lanes == 0, 0.0, pltpu.roll(sums[0], 1, 1))
                    left = jnp.where(lanes == width - 1, 0.0, pltpu.roll(sums[2], width - 1, 1))
                    mixed[r, at, :] = (sums[1] + right + left).astype(BF16)

    mix([(1, rows + 1)])

    acc[...] = jnp.zeros_like(acc)

    @pl.loop(0, rows, unroll=4)
    def _(r):
        q = mixed[r + 1, 0:channels, :]
        k = mixed[r + 1, channels : 2 * channels, :]
        v = mixed[r + 1, 2 * channels : 3 * channels, :]
        acc[0, :, 0:channels] += dot(q, k, NT)
        acc[1, :, 0:channels] += dot(ga[r + 1], v, NT)
        qf = q.astype(F32)
        kf = k.astype(F32)
        acc[3] += qf * qf
        acc[4] += kf * kf

    each = gram.shape[1]
    owners = gram.shape[0]
    gram_rows = owners * each
    pieces = []
    for h in range(heads):
        a, b = 48 * h, 48 * (h + 1)
        qsq = jnp.sum(acc[3, a:b, :], axis=1, keepdims=True)
        ksq = jnp.sum(acc[4, a:b, :], axis=1, keepdims=True)
        pieces.append(
            jnp.concatenate(
                [acc[0, a:b, a:b], acc[1, a:b, a:b], qsq, ksq, jnp.zeros((48, 30), F32)], axis=1,
            )
        )
    if gram_rows > channels:
        pieces.append(jnp.zeros((gram_rows - channels, 128), F32))
    packed = jnp.concatenate(pieces, axis=0)
    for i in range(owners):
        gram[i] = packed[i * each : (i + 1) * each]

    owner = tile < owners
    rest = pl.ds(0, n_tile - 1)

    @pl.loop(1, n_tile)
    def _(d):
        p = lax.rem(tile + d, n_tile)

        @pl.when(p < owners)
        def _():
            remote(gram.at[p], gram_recv.at[tile], gram_rs, {"img": img, "tile": p}).start()

    @pl.when(has_lo)
    def _():
        to_next()[1].wait_recv()
        proj[0] = project(lo[0])
        ga[0] = dot(om_t[...], lo[2]).astype(BF16)

    @pl.when(has_hi)
    def _():
        to_previous()[1].wait_recv()
        proj[rows + 3] = project(hi[1])
        ga[rows + 1] = dot(om_t[...], hi[2]).astype(BF16)

    mix([(0, 1), (rows + 1, rows + 2)])

    @pl.when(owner)
    def _():
        gram_recv[tile] = gram[tile]
        wait_bytes(gram_recv.at[rest], gram_rs.at[1])

        def add_gram(i, total):
            return total + gram_recv[i]

        gram_all[tile] = lax.fori_loop(0, n_tile, add_gram, jnp.zeros(gram.shape[1:], F32))

        @pl.loop(1, n_tile)
        def _(d):
            p = lax.rem(tile + d, n_tile)
            remote(gram_all.at[tile], gram_all.at[tile], gram_ag, {"img": img, "tile": p}).start()

    gg_ref[...] = jnp.zeros_like(gg_ref)
    ggt_ref[...] = jnp.zeros_like(ggt_ref)
    at_ref[...] = jnp.zeros_like(at_ref)
    extra[...] = jnp.zeros_like(extra)
    sacc[...] = jnp.zeros_like(sacc)

    @pl.loop(0, rows, unroll=4)
    def _(r):
        acc[2, :, 0:channels] += dot(cot_ref[r], mixed[r + 1, 2 * channels : 3 * channels, :], NT)


    @pl.when(owner)
    def _():
        wait_bytes(gram_all.at[pl.ds(0, owners - 1)], gram_ag.at[1])

    @pl.when(jnp.logical_not(owner))
    def _():
        wait_bytes(gram_all, gram_ag.at[1])

    whole = jnp.concatenate([gram_all[i] for i in range(owners)], axis=0)

    eye = lax.broadcasted_iota(jnp.int32, (48, 48), 0) == lax.broadcasted_iota(
        jnp.int32, (48, 48), 1
    )
    lane = lax.broadcasted_iota(jnp.int32, (1, 128), 1)
    leading = (tile == 0).astype(F32)
    for h in range(heads):
        a, b = 48 * h, 48 * (h + 1)
        gram_raw = whole[a:b, 0:48]
        grad_att = whole[a:b, 48:96]
        qsq = whole[a:b, 96:97]
        ksq_col = whole[a:b, 97:98]
        ksq = jnp.sum(jnp.where(eye, ksq_col, 0.0), axis=0, keepdims=True)
        lengths = jnp.sqrt(qsq + 1e-06) * jnp.sqrt(ksq + 1e-06)
        cosine = gram_raw / lengths
        e = jnp.exp(cosine * sharp_ref[h])
        attention = e / jnp.sum(e, axis=1, keepdims=True)
        grad_scores = attention * (grad_att - jnp.sum(attention * grad_att, axis=1, keepdims=True))
        sharp_sum = leading * jnp.sum(
            jnp.sum(grad_scores * cosine, axis=1, keepdims=True), axis=0, keepdims=True
        )
        extra[3 * channels : 3 * channels + 1, :] += jnp.where(lane == 64 + h, sharp_sum, 0.0)
        grad_cos = grad_scores * sharp_ref[h]
        gg = grad_cos / lengths
        terms = grad_cos * cosine
        gg_ref[a:b, a:b] = gg.astype(BF16)
        ggt_ref[a:b, a:b] = gg.T.astype(BF16)
        at_ref[a:b, a:b] = attention.T.astype(BF16)
        coef[a:b, 0:1] = jnp.sum(terms, axis=1, keepdims=True) / (qsq + 1e-06)
        kc = jnp.sum(terms, axis=0, keepdims=True) / (ksq + 1e-06)
        coef[a:b, 1:2] = jnp.sum(jnp.where(eye, kc, 0.0), axis=1, keepdims=True)

    oma = dot(acc[2, :, 0:channels].astype(BF16), at_ref[...])

    qc = coef[:, 0:1]
    kc = coef[:, 1:2]

    @pl.loop(0, rows + 2, unroll=5)
    def _(r):
        inside = jnp.logical_and(
            jnp.logical_or(r > 0, has_lo), jnp.logical_or(r < rows + 1, has_hi)
        ).astype(F32)
        q = mixed[r, 0:channels, :]
        k = mixed[r, channels : 2 * channels, :]
        gq = dot(gg_ref[...], k) - q.astype(F32) * qc
        gk = dot(ggt_ref[...], q) - k.astype(F32) * kc
        gv = dot(at_ref[...], ga[r])
        gm[r, 0:channels, :] = (gq * inside).astype(BF16)
        gm[r, channels : 2 * channels, :] = (gk * inside).astype(BF16)
        gm[r, 2 * channels : 3 * channels, :] = (gv * inside).astype(BF16)

    lane_g = lax.broadcasted_iota(jnp.int32, (group, 128), 1)

    @pl.loop(0, 3 * channels // group, unroll=2)
    def _(g):
        at = pl.ds(pl.multiple_of(g * group, group), group)
        weights = stencil_ref[at, :]
        w = [jnp.broadcast_to(weights[:, t : t + 1], (group, width)) for t in range(9)]
        line = [gm[i, at, :].astype(F32) for i in range(2)]
        for r in range(rows):
            line.append(gm[r + 2, at, :].astype(F32))
            sums = [
                w[b] * line[r + 2] + w[3 + b] * line[r + 1] + w[6 + b] * line[r] for b in range(3)
            ]
            left = jnp.where(lanes == width - 1, 0.0, pltpu.roll(sums[0], width - 1, 1))
            right = jnp.where(lanes == 0, 0.0, pltpu.roll(sums[2], 1, 1))
            gp[r, at, :] = (sums[1] + right + left).astype(BF16)

    @pl.loop(0, 3 * channels // group, unroll=2)
    def _(g):
        at = pl.ds(pl.multiple_of(g * group, group), group)
        tap = [jnp.zeros((group, 128), F32) for _ in range(9)]
        line = [proj[1 + i, at, :].astype(F32) for i in range(2)]
        for r in range(rows):
            line.append(proj[r + 3, at, :].astype(F32))
            g_mid = gm[r + 1, at, :].astype(F32)
            right, left = shifted(g_mid, lanes)
            for a in range(3):
                for b, side in enumerate((left, g_mid, right)):
                    for c in range(0, width, 128):
                        tap[3 * a + b] += line[r + a][:, c : c + 128] * side[:, c : c + 128]
        total = jnp.zeros((group, 128), F32)
        for t in range(9):
            s = jnp.sum(tap[t], axis=1, keepdims=True)
            total = total + jnp.where(lane_g == 72 + t, s, 0.0)
        extra[at, :] = total

    @pl.loop(0, rows, unroll=4)
    def _(r):
        sacc[...] += dot(gp[r], ext[r], NT)

    n1 = 3 * channels
    n2 = 4 * channels
    groups, piece = half.shape[:2]
    tail = sacc[:, 128:256]
    tail_lane = lax.broadcasted_iota(jnp.int32, tail.shape, 1)
    tail = jnp.where(tail_lane <= 64, tail, 0.0)
    mixer_f = mixer_ref[...].astype(F32)
    scaling_part = jnp.sum(mixer_f * sacc[:, 0:channels], axis=0, keepdims=True)
    oma_lane = lax.broadcasted_iota(jnp.int32, (channels, 128), 1)
    oma_tail = jnp.concatenate([oma[:, 128:192], jnp.zeros((channels, 64), F32)], axis=1)
    oma_tail = oma_tail + jnp.where(oma_lane == 72, column(scaling_part), 0.0)

    def split_again(x):
        at = lax.broadcasted_iota(jnp.int32, x.shape, x.ndim - 1)
        both = x + pltpu.roll(x, 96, x.ndim - 1)
        high = both.astype(BF16).astype(F32)
        low = pltpu.roll(both - high, 32, x.ndim - 1)
        return jnp.where(at < 64, x, jnp.where(at < 96, high, low))

    spare = groups * piece - n2
    filler = [jnp.zeros((spare, 128), BF16)] if spare else []
    head_part = [sacc[:, 0:128].astype(BF16), oma[:, 0:128].astype(BF16)] + filler
    tail_part = [
        split_again(tail + extra[0:n1, :]).astype(BF16),
        split_again(oma_tail + extra[n1:, :]).astype(BF16),
    ] + filler
    red[0] = jnp.concatenate(head_part, axis=0).reshape(half.shape)
    red[1] = jnp.concatenate(tail_part, axis=0).reshape(half.shape)

    core = lax.rem(tile, 2)
    place = lax.div(me, 2)
    partner = {"img": img, "tile": tile + 1 - 2 * core}
    others = pl.ds(0, groups - 1)

    def feature_rows(first_row, last_row):
        @pl.loop(first_row, last_row, unroll=min(last_row - first_row, 4))
        def _(r):
            standard = std32[r]
            inverse = inv[r]
            scaled = dot(mixer_t[...], gp[r]) * scale
            first = jnp.mean(scaled, axis=0, keepdims=True)
            second = jnp.mean(scaled * standard, axis=0, keepdims=True)
            adjoint = cot_ref[r].astype(F32) + (scaled - first - standard * second) * inverse
            for c in range(width // 128):
                own32[pl.ds(c * channels * rows + r, channels, stride=rows), :] = adjoint[
                    :, 128 * c : 128 * c + 128
                ]

    swap = remote(red.at[1 - core], pair, pair_rs, partner)
    swap.start()
    feature_rows(0, 2)
    swap.wait_recv()

    def rounded(x):
        return jnp.where(core == 1, split_again(x), x).astype(BF16)

    def add_pair(i, _):
        half[i] = rounded(red[core, i].astype(F32) + pair[i].astype(F32))
        return 0

    lax.fori_loop(0, groups, add_pair, 0)

    @pl.loop(1, groups)
    def _(d):
        p = lax.rem(place + d, groups)
        remote(half.at[p], recv.at[place], main_rs, device(2 * p + core)).start()

    recv[place] = half[place]

    feature_rows(2, 6)
    wait_bytes(recv.at[others], main_rs.at[1])

    def add(i, total):
        return total + recv[i].astype(F32)

    total = lax.fori_loop(0, groups, add, jnp.zeros(recv.shape[1:], F32))
    gath[core, place] = rounded(total)

    @pl.loop(1, groups)
    def _(d):
        p = lax.rem(place + d, groups)
        pltpu.make_async_remote_copy(
            src_ref=gath.at[core, place], dst_ref=gath.at[core, place], send_sem=ag_send,
            recv_sem=ag_recv.at[place], device_id=device(2 * p + core),
            device_id_type=pl.DeviceIdType.MESH,
        ).start()

    remote(gath.at[core, place], gath.at[core, place], pair_ag, partner).start()
    feature_rows(6, rows)
    for c in range(width // 128):
        part = own32[pl.ds(c * channels * rows, channels * rows), :]
        out_ref[:, :, 128 * c : 128 * c + 128] = part.reshape(channels, rows, 128).astype(BF16)

    @pl.loop(1, groups)
    def _(d):
        p = lax.rem(place + groups - d, groups)
        wait_bytes(gath.at[core, p], ag_recv.at[p])
        remote(gath.at[core, p], gath.at[core, p], pair_ag, partner).start()

    wait_bytes(gath.at[1 - core], pair_ag.at[1])

    gath_out[...] = gath[...]

    @pl.when(has_hi)
    def _():
        for copy in to_next():
            copy.wait_send()

    @pl.when(has_lo)
    def _():
        for copy in to_previous():
            copy.wait_send()

    @pl.when(owner)
    def _():
        wait_bytes(gram.at[pl.ds(0, owners - 1)], gram_rs.at[0])
        wait_bytes(gram_recv.at[rest], gram_ag.at[0])

    @pl.when(jnp.logical_not(owner))
    def _():
        wait_bytes(gram, gram_rs.at[0])

    swap.wait_send()
    wait_bytes(recv.at[others], main_rs.at[0])
    wait_bytes(half.at[others], ag_send)
    wait_bytes(gath.at[core], pair_ag.at[0])


def finish_kernel(
    adjoint_ref, gath_ref, mixer_t, scale_ref, offset_ref,
    out_ref, triple_ref, stencil_ref, outgoing_ref, sharp_ref, scaling_ref, offset_out_ref, sem,
):
    move = pltpu.make_async_copy(adjoint_ref, out_ref, sem)
    move.start()
    channels, n1 = mixer_t.shape
    n2 = n1 + channels
    left = gath_ref[0].reshape(-1, 128).astype(F32)
    right = gath_ref[1].reshape(-1, 128).astype(F32)
    full = right + pltpu.roll(right, 96, 1)
    s = jnp.concatenate([left[0:n1], right[0:n1, 0:64]], axis=1)
    gsum = full[0:n1, 64:65]
    triple_ref[...] = (s * scale_ref[...] + gsum * offset_ref[...]).T
    turned = full[0:n1].T
    for t in range(9):
        stencil_ref[t // 3, t % 3 : t % 3 + 1, :] = turned[72 + t : 73 + t, :]
    outgoing_ref[...] = jnp.concatenate([left[n1:n2], right[n1:n2, 0:64]], axis=1)
    sharp_ref[...] = full[n1 : n1 + 1, 64:68]
    scaling_ref[...] = full[n1:n2].T[72:73, :]
    mixer = mixer_t[...].T.astype(F32)
    offset_out_ref[...] = jnp.sum(mixer * gsum, axis=0, keepdims=True)
    move.wait()


def local(
    block_feature_map, upstream_sensitivity, triple_mixer, spatial_stencil, outgoing_mixer,
    sharpness_factor, standardize_scaling, standardize_offset,
):
    _, channels, rows, width = block_feature_map.shape
    n_img = lax.axis_size("img")
    n_tile = lax.axis_size("tile")
    groups = n_img * n_tile // 2
    n1 = 3 * channels
    each = -(-channels // (n_tile * 8)) * 8
    owners = -(-channels // each)
    piece = -(-4 * channels // (groups * 16)) * 16

    shape = jax.ShapeDtypeStruct
    vmem = pltpu.VMEM
    pair_sem = pltpu.SemaphoreType.DMA((2,))
    mixer_t = triple_mixer.T
    scale_row = standardize_scaling.reshape(1, channels)
    offset_row = standardize_offset.reshape(1, channels)
    adjoint, gathered = pl.pallas_call(
        functools.partial(kernel, n_img, n_tile),
        out_shape=(
            shape((channels, rows, width), BF16),
            shape((2, groups, piece, 128), BF16),
        ),
        in_specs=[VMEM] * 7 + [SMEM],
        out_specs=[VMEM] * 2,
        scratch_shapes=[
            vmem((channels * rows * width // 128, 128), F32),
            vmem((channels * rows * width // 128, 128), F32),
            vmem((rows, channels, width), F32),
            vmem((rows, 256, width), BF16),
            vmem((rows, 1, width), F32),
            vmem((rows, channels, width), BF16),
            vmem((rows, channels, width), BF16),
            vmem((n1, channels), BF16),
            vmem((channels, channels), BF16),
            vmem((n1, 128), F32),
            vmem((3, channels, width), BF16),
            vmem((3, channels, width), BF16),
            vmem((rows + 4, n1, width), BF16),
            vmem((rows + 2, n1, width), BF16),
            vmem((rows + 2, channels, width), BF16),
            vmem((rows + 2, n1, width), BF16),
            vmem((rows, n1, width), BF16),
            vmem((5, channels, 256), F32),
            vmem((owners, each, 128), F32),
            vmem((n_tile, each, 128), F32),
            vmem((owners, each, 128), F32),
            vmem((channels, channels), BF16),
            vmem((channels, channels), BF16),
            vmem((channels, channels), BF16),
            vmem((channels, 128), F32),
            vmem((n1, 256), F32),
            vmem((4 * channels, 128), F32),
            vmem((2, groups, piece, 128), BF16),
            vmem((groups, piece, 128), BF16),
            vmem((groups, piece, 128), BF16),
            vmem((groups, piece, 128), BF16),
            vmem((2, groups, piece, 128), BF16),
        ]
        + [pair_sem] * 9
        + [pltpu.SemaphoreType.DMA, pltpu.SemaphoreType.DMA((groups,))],
        compiler_params=pltpu.CompilerParams(
            collective_id=0, has_side_effects=True, vmem_limit_bytes=LIMIT
        ),
        name="block",
    )(
        block_feature_map[0], upstream_sensitivity[0], mixer_t,
        jnp.transpose(spatial_stencil, (1, 2, 0)), outgoing_mixer, scale_row, offset_row,
        sharpness_factor,
    )
    anywhere = pl.BlockSpec(memory_space=pl.ANY)
    out, triple, stencil, outgoing, sharp, scaling, offset = pl.pallas_call(
        finish_kernel,
        out_shape=(
            shape((channels, rows, width), BF16),
            shape((channels, n1), F32),
            shape((3, 3, n1), F32),
            shape((channels, channels), F32),
            shape((1, sharpness_factor.shape[0]), F32),
            shape((1, channels), F32),
            shape((1, channels), F32),
        ),
        in_specs=[anywhere] + [VMEM] * 4,
        out_specs=[anywhere] + [VMEM] * 6,
        scratch_shapes=[pltpu.SemaphoreType.DMA],
        compiler_params=pltpu.CompilerParams(vmem_limit_bytes=LIMIT),
        name="finish",
    )(adjoint, gathered, mixer_t, scale_row, offset_row)
    return (
        out[None],
        triple.T,
        jnp.transpose(stencil, (2, 0, 1)),
        outgoing,
        sharp[0],
        scaling[0],
        offset[0],
    )


def solution(mesh):
    rows = P("img", None, "tile", None)
    return jax.shard_map(
        local,
        mesh=mesh,
        in_specs=(rows, rows, P(), P(), P(), P(), P(), P()),
        out_specs=(rows, P(), P(), P(), P(), P(), P()),
        check_vma=False,
    )
```

```python
import functools
import jax
import jax.numpy as jnp
from jax import lax
from jax.experimental import pallas as pl
from jax.experimental.pallas import tpu as pltpu
from jax.sharding import PartitionSpec as P

F32 = jnp.float32
BF16 = jnp.bfloat16
NT = (((1,), (1,)), ((), ()))
NN = (((1,), (0,)), ((), ()))
TN = (((0,), (0,)), ((), ()))
VMEM = pl.BlockSpec(memory_space=pltpu.VMEM)
SMEM = pl.BlockSpec(memory_space=pltpu.SMEM)
LIMIT = 56 * 1024 * 1024


def dot(a, b, dims=NN):
    return lax.dot_general(a, b, dims, preferred_element_type=F32)


def standardized(x):
    xf = x.astype(F32)
    centered = xf - jnp.mean(xf, axis=0, keepdims=True)
    inverse = lax.rsqrt(jnp.mean(centered * centered, axis=0, keepdims=True) + 1e-05)
    return centered * inverse, inverse


def shifted(v, lanes):
    width = v.shape[-1]
    right = jnp.where(lanes == 0, 0.0, pltpu.roll(v, 1, 1))
    left = jnp.where(lanes == width - 1, 0.0, pltpu.roll(v, width - 1, 1))
    return right, left


def column_sums(w, line):
    return [
        jnp.concatenate(
            [
                w[b] * line[0][:, c : c + 128]
                + w[3 + b] * line[1][:, c : c + 128]
                + w[6 + b] * line[2][:, c : c + 128]
                for c in range(0, line[0].shape[1], 128)
            ],
            axis=1,
        )
        for b in range(3)
    ]


def column(row):
    n = row.shape[1]
    eye = lax.broadcasted_iota(jnp.int32, (n, n), 0) == lax.broadcasted_iota(jnp.int32, (n, n), 1)
    return jnp.sum(jnp.where(eye, row, 0.0), axis=1, keepdims=True)


def remote(src, dst, sems, ids):
    return pltpu.make_async_remote_copy(
        src_ref=src, dst_ref=dst, send_sem=sems.at[0], recv_sem=sems.at[1], device_id=ids,
        device_id_type=pl.DeviceIdType.MESH,
    )


def wait_bytes(ref, sem):
    pltpu.make_async_copy(ref, ref, sem).wait()


def kernel(
    n_img, n_tile,
    own_in, cot_in, mixer_t, stencil_in, out_mixer_ref, scale_ref, offset_ref, sharp_ref,
    out_ref, gath_out,
    wide, own32, cot32, std32, ext, inv, own_ref, cot_ref, mixer_ref, om_t, stencil_ref, lo, hi, proj, mixed, ga, gm, gp, acc, gram, gram_recv, gram_all, gg_ref, ggt_ref, at_ref, coef,
    sacc, extra, red, pair, half, recv, gath,
    lo_x, lo_c, hi_x, hi_c, gram_rs, gram_ag, pair_rs, main_rs, pair_ag, ag_send, ag_recv,
):
    channels, rows, width = own_in.shape
    heads = channels // 48
    img = lax.axis_index("img")
    tile = lax.axis_index("tile")
    n = n_img * n_tile
    me = img * n_tile + tile

    def device(p):
        return {"img": lax.div(p, n_tile), "tile": lax.rem(p, n_tile)}

    barrier = pltpu.get_barrier_semaphore()

    @pl.loop(1, n)
    def _(d):
        pl.semaphore_signal(
            barrier, inc=1, device_id=device(lax.rem(me + d, n)),
            device_id_type=pl.DeviceIdType.MESH,
        )

    def line_of(ref, r):
        return jnp.concatenate(
            [ref[pl.ds(c * channels * rows + r, channels, stride=rows), :] for c in range(width // 128)],
            axis=1,
        )

    for c in range(width // 128):
        part = pl.ds(c * channels * rows, channels * rows)
        cols = slice(128 * c, 128 * c + 128)
        own32[part, :] = own_in[:, :, cols].astype(F32).reshape(channels * rows, 128)
        cot32[part, :] = cot_in[:, :, cols].astype(F32).reshape(channels * rows, 128)
    for r in range(rows):
        own_ref[r] = line_of(own32, r).astype(BF16)
        cot_ref[r] = line_of(cot32, r).astype(BF16)

    mixer_ref[...] = mixer_t[...].T
    om_t[...] = out_mixer_ref[...].T
    taps = jnp.concatenate(
        [stencil_in[t // 3, t % 3 : t % 3 + 1, :] for t in range(9)]
        + [jnp.zeros((119, 3 * channels), F32)], axis=0,
    )
    stencil_ref[...] = taps.T

    pl.semaphore_wait(barrier, n - 1)

    def to_next():
        ids = {"img": img, "tile": tile + 1}
        return (
            remote(own_ref.at[pl.ds(rows - 2, 2)], lo.at[pl.ds(0, 2)], lo_x, ids),
            remote(cot_ref.at[pl.ds(rows - 1, 1)], lo.at[pl.ds(2, 1)], lo_c, ids),
        )

    def to_previous():
        ids = {"img": img, "tile": tile - 1}
        return (
            remote(own_ref.at[pl.ds(0, 2)], hi.at[pl.ds(0, 2)], hi_x, ids),
            remote(cot_ref.at[pl.ds(0, 1)], hi.at[pl.ds(2, 1)], hi_c, ids),
        )

    has_lo = tile > 0
    has_hi = tile < n_tile - 1

    @pl.when(has_hi)
    def _():
        for copy in to_next():
            copy.start()

    @pl.when(has_lo)
    def _():
        for copy in to_previous():
            copy.start()

    wide[0] = jnp.broadcast_to(column(scale_ref[...]), (channels, 128))
    wide[1] = jnp.broadcast_to(column(offset_ref[...]), (channels, 128))
    halves = [slice(c, c + 128) for c in range(0, width, 128)]

    def project(x):
        parts = []
        for c in halves:
            standard, _ = standardized(x[:, c])
            parts.append((standard * wide[0] + wide[1]).astype(BF16))
        return dot(mixer_ref[...], jnp.concatenate(parts, axis=1)).astype(BF16)

    @pl.loop(0, rows)
    def _(r):
        parts = []
        for c in halves:
            standard, inverse = standardized(own_ref[r, :, c])
            std32[r, :, c] = standard
            inv[r, :, c] = inverse
            ext[r, 0:channels, c] = standard.astype(BF16)
            parts.append((standard * wide[0] + wide[1]).astype(BF16))
        ext[r, channels:256, :] = jnp.ones((256 - channels, width), BF16)
        proj[r + 2] = dot(mixer_ref[...], jnp.concatenate(parts, axis=1)).astype(BF16)
        ga[r + 1] = dot(om_t[...], cot_ref[r]).astype(BF16)

    @pl.when(has_lo)
    def _():
        to_next()[0].wait_recv()
        proj[1] = project(lo[1])

    @pl.when(jnp.logical_not(has_lo))
    def _():
        proj[0:2] = jnp.zeros((2,) + proj.shape[1:], BF16)
        ga[0] = jnp.zeros(ga.shape[1:], BF16)

    @pl.when(has_hi)
    def _():
        to_previous()[0].wait_recv()
        proj[rows + 2] = project(hi[0])

    @pl.when(jnp.logical_not(has_hi))
    def _():
        proj[rows + 2 : rows + 4] = jnp.zeros((2,) + proj.shape[1:], BF16)
        ga[rows + 1] = jnp.zeros(ga.shape[1:], BF16)

    group = 16
    lanes = lax.broadcasted_iota(jnp.int32, (group, width), 1)

    def mix(strips):
        @pl.loop(0, 3 * channels // group)
        def _(g):
            at = pl.ds(pl.multiple_of(g * group, group), group)
            weights = stencil_ref[at, :]
            w = [jnp.broadcast_to(weights[:, t : t + 1], (group, 128)) for t in range(9)]
            for first_row, last_row in strips:
                line = [proj[first_row + i, at, :].astype(F32) for i in range(2)]
                for r in range(first_row, last_row):
                    line = line[-2:] + [proj[r + 2, at, :].astype(F32)]
                    sums = column_sums(w, line)
                    right = jnp.where(lanes == 0, 0.0, pltpu.roll(sums[0], 1, 1))
                    left = jnp.where(lanes == width - 1, 0.0, pltpu.roll(sums[2], width - 1, 1))
                    mixed[r, at, :] = (sums[1] + right + left).astype(BF16)

    mix([(1, rows + 1)])

    acc[...] = jnp.zeros_like(acc)

    @pl.loop(0, rows)
    def _(r):
        q = mixed[r + 1, 0:channels, :]
        k = mixed[r + 1, channels : 2 * channels, :]
        v = mixed[r + 1, 2 * channels : 3 * channels, :]
        acc[0, :, 0:channels] += dot(q, k, NT)
        acc[1, :, 0:channels] += dot(ga[r + 1], v, NT)
        qf = q.astype(F32)
        kf = k.astype(F32)
        acc[3] += qf * qf
        acc[4] += kf * kf

    each = gram.shape[1]
    owners = gram.shape[0]
    gram_rows = owners * each
    pieces = []
    for h in range(heads):
        a, b = 48 * h, 48 * (h + 1)
        qsq = jnp.sum(acc[3, a:b, :], axis=1, keepdims=True)
        ksq = jnp.sum(acc[4, a:b, :], axis=1, keepdims=True)
        pieces.append(
            jnp.concatenate(
                [acc[0, a:b, a:b], acc[1, a:b, a:b], qsq, ksq, jnp.zeros((48, 30), F32)], axis=1,
            )
        )
    if gram_rows > channels:
        pieces.append(jnp.zeros((gram_rows - channels, 128), F32))
    packed = jnp.concatenate(pieces, axis=0)
    for i in range(owners):
        gram[i] = packed[i * each : (i + 1) * each]

    owner = tile < owners
    rest = pl.ds(0, n_tile - 1)

    @pl.loop(1, n_tile)
    def _(d):
        p = lax.rem(tile + d, n_tile)

        @pl.when(p < owners)
        def _():
            remote(gram.at[p], gram_recv.at[tile], gram_rs, {"img": img, "tile": p}).start()

    @pl.when(has_lo)
    def _():
        to_next()[1].wait_recv()
        proj[0] = project(lo[0])
        ga[0] = dot(om_t[...], lo[2]).astype(BF16)

    @pl.when(has_hi)
    def _():
        to_previous()[1].wait_recv()
        proj[rows + 3] = project(hi[1])
        ga[rows + 1] = dot(om_t[...], hi[2]).astype(BF16)

    mix([(0, 1), (rows + 1, rows + 2)])

    @pl.when(owner)
    def _():
        gram_recv[tile] = gram[tile]
        wait_bytes(gram_recv.at[rest], gram_rs.at[1])

        def add_gram(i, total):
            return total + gram_recv[i]

        gram_all[tile] = lax.fori_loop(0, n_tile, add_gram, jnp.zeros(gram.shape[1:], F32))

        @pl.loop(1, n_tile)
        def _(d):
            p = lax.rem(tile + d, n_tile)
            remote(gram_all.at[tile], gram_all.at[tile], gram_ag, {"img": img, "tile": p}).start()

    gg_ref[...] = jnp.zeros_like(gg_ref)
    ggt_ref[...] = jnp.zeros_like(ggt_ref)
    at_ref[...] = jnp.zeros_like(at_ref)
    extra[...] = jnp.zeros_like(extra)
    sacc[...] = jnp.zeros_like(sacc)

    @pl.loop(0, rows)
    def _(r):
        acc[2, :, 0:channels] += dot(cot_ref[r], mixed[r + 1, 2 * channels : 3 * channels, :], NT)


    @pl.when(owner)
    def _():
        wait_bytes(gram_all.at[pl.ds(0, owners - 1)], gram_ag.at[1])

    @pl.when(jnp.logical_not(owner))
    def _():
        wait_bytes(gram_all, gram_ag.at[1])

    whole = jnp.concatenate([gram_all[i] for i in range(owners)], axis=0)

    eye = lax.broadcasted_iota(jnp.int32, (48, 48), 0) == lax.broadcasted_iota(
        jnp.int32, (48, 48), 1
    )
    lane = lax.broadcasted_iota(jnp.int32, (1, 128), 1)
    leading = (tile == 0).astype(F32)
    for h in range(heads):
        a, b = 48 * h, 48 * (h + 1)
        gram_raw = whole[a:b, 0:48]
        grad_att = whole[a:b, 48:96]
        qsq = whole[a:b, 96:97]
        ksq_col = whole[a:b, 97:98]
        ksq = jnp.sum(jnp.where(eye, ksq_col, 0.0), axis=0, keepdims=True)
        lengths = jnp.sqrt(qsq + 1e-06) * jnp.sqrt(ksq + 1e-06)
        cosine = gram_raw / lengths
        e = jnp.exp(cosine * sharp_ref[h])
        attention = e / jnp.sum(e, axis=1, keepdims=True)
        grad_scores = attention * (grad_att - jnp.sum(attention * grad_att, axis=1, keepdims=True))
        sharp_sum = leading * jnp.sum(
            jnp.sum(grad_scores * cosine, axis=1, keepdims=True), axis=0, keepdims=True
        )
        extra[3 * channels : 3 * channels + 1, :] += jnp.where(lane == 64 + h, sharp_sum, 0.0)
        grad_cos = grad_scores * sharp_ref[h]
        gg = grad_cos / lengths
        terms = grad_cos * cosine
        gg_ref[a:b, a:b] = gg.astype(BF16)
        ggt_ref[a:b, a:b] = gg.T.astype(BF16)
        at_ref[a:b, a:b] = attention.T.astype(BF16)
        coef[a:b, 0:1] = jnp.sum(terms, axis=1, keepdims=True) / (qsq + 1e-06)
        kc = jnp.sum(terms, axis=0, keepdims=True) / (ksq + 1e-06)
        coef[a:b, 1:2] = jnp.sum(jnp.where(eye, kc, 0.0), axis=1, keepdims=True)

    oma = dot(acc[2, :, 0:channels].astype(BF16), at_ref[...])

    wide[2] = jnp.broadcast_to(coef[:, 0:1], (channels, 128))
    wide[3] = jnp.broadcast_to(coef[:, 1:2], (channels, 128))

    @pl.loop(0, rows + 2)
    def _(r):
        inside = jnp.logical_and(
            jnp.logical_or(r > 0, has_lo), jnp.logical_or(r < rows + 1, has_hi)
        ).astype(F32)
        q = mixed[r, 0:channels, :]
        k = mixed[r, channels : 2 * channels, :]
        gq = dot(gg_ref[...], k)
        for c in halves:
            gm[r, 0:channels, c] = ((gq[:, c] - q[:, c].astype(F32) * wide[2]) * inside).astype(BF16)
        gk = dot(ggt_ref[...], q)
        for c in halves:
            gm[r, channels : 2 * channels, c] = (
                (gk[:, c] - k[:, c].astype(F32) * wide[3]) * inside
            ).astype(BF16)
        gv = dot(at_ref[...], ga[r])
        gm[r, 2 * channels : 3 * channels, :] = (gv * inside).astype(BF16)

    lane_g = lax.broadcasted_iota(jnp.int32, (group, 128), 1)

    @pl.loop(0, 3 * channels // group)
    def _(g):
        at = pl.ds(pl.multiple_of(g * group, group), group)
        weights = stencil_ref[at, :]
        w = [jnp.broadcast_to(weights[:, t : t + 1], (group, 128)) for t in range(9)]
        line = [gm[i, at, :].astype(F32) for i in range(2)]
        for r in range(rows):
            line.append(gm[r + 2, at, :].astype(F32))
            sums = column_sums(w, line[r : r + 3][::-1])
            left = jnp.where(lanes == width - 1, 0.0, pltpu.roll(sums[0], width - 1, 1))
            right = jnp.where(lanes == 0, 0.0, pltpu.roll(sums[2], 1, 1))
            gp[r, at, :] = (sums[1] + right + left).astype(BF16)

    @pl.loop(0, 3 * channels // group)
    def _(g):
        at = pl.ds(pl.multiple_of(g * group, group), group)
        tap = [jnp.zeros((group, 128), F32) for _ in range(9)]
        line = [proj[1 + i, at, :].astype(F32) for i in range(2)]
        for r in range(rows):
            line.append(proj[r + 3, at, :].astype(F32))
            g_mid = gm[r + 1, at, :].astype(F32)
            right, left = shifted(g_mid, lanes)
            for a in range(3):
                for b, side in enumerate((left, g_mid, right)):
                    for c in range(0, width, 128):
                        tap[3 * a + b] += line[r + a][:, c : c + 128] * side[:, c : c + 128]
        total = jnp.zeros((group, 128), F32)
        for t in range(9):
            s = jnp.sum(tap[t], axis=1, keepdims=True)
            total = total + jnp.where(lane_g == 72 + t, s, 0.0)
        extra[at, :] = total

    @pl.loop(0, rows)
    def _(r):
        sacc[...] += dot(gp[r], ext[r], NT)

    n1 = 3 * channels
    n2 = 4 * channels
    groups, piece = half.shape[:2]
    tail = sacc[:, 128:256]
    tail_lane = lax.broadcasted_iota(jnp.int32, tail.shape, 1)
    tail = jnp.where(tail_lane <= 64, tail, 0.0)
    mixer_f = mixer_ref[...].astype(F32)
    scaling_part = jnp.sum(mixer_f * sacc[:, 0:channels], axis=0, keepdims=True)
    oma_lane = lax.broadcasted_iota(jnp.int32, (channels, 128), 1)
    oma_tail = jnp.concatenate([oma[:, 128:192], jnp.zeros((channels, 64), F32)], axis=1)
    oma_tail = oma_tail + jnp.where(oma_lane == 72, column(scaling_part), 0.0)

    def split_again(x):
        at = lax.broadcasted_iota(jnp.int32, x.shape, x.ndim - 1)
        both = x + pltpu.roll(x, 96, x.ndim - 1)
        high = both.astype(BF16).astype(F32)
        low = pltpu.roll(both - high, 32, x.ndim - 1)
        return jnp.where(at < 64, x, jnp.where(at < 96, high, low))

    spare = groups * piece - n2
    filler = [jnp.zeros((spare, 128), BF16)] if spare else []
    head_part = [sacc[:, 0:128].astype(BF16), oma[:, 0:128].astype(BF16)] + filler
    tail_part = [
        split_again(tail + extra[0:n1, :]).astype(BF16),
        split_again(oma_tail + extra[n1:, :]).astype(BF16),
    ] + filler
    red[0] = jnp.concatenate(head_part, axis=0).reshape(half.shape)
    red[1] = jnp.concatenate(tail_part, axis=0).reshape(half.shape)

    core = lax.rem(tile, 2)
    place = lax.div(me, 2)
    partner = {"img": img, "tile": tile + 1 - 2 * core}
    others = pl.ds(0, groups - 1)

    def feature_rows(first_row, last_row):
        @pl.loop(first_row, last_row)
        def _(r):
            grad_normed = dot(mixer_t[...], gp[r])
            for i, c in enumerate(halves):
                standard = std32[r, :, c]
                scaled = grad_normed[:, c] * wide[0]
                first = jnp.mean(scaled, axis=0, keepdims=True)
                second = jnp.mean(scaled * standard, axis=0, keepdims=True)
                own32[pl.ds(i * channels * rows + r, channels, stride=rows), :] = cot_ref[
                    r, :, c
                ].astype(F32) + (scaled - first - standard * second) * inv[r, :, c]

    swap = remote(red.at[1 - core], pair, pair_rs, partner)
    swap.start()
    feature_rows(0, 2)
    swap.wait_recv()

    def rounded(x):
        return jnp.where(core == 1, split_again(x), x).astype(BF16)

    def add_pair(i, _):
        half[i] = rounded(red[core, i].astype(F32) + pair[i].astype(F32))
        return 0

    lax.fori_loop(0, groups, add_pair, 0)

    @pl.loop(1, groups)
    def _(d):
        p = lax.rem(place + d, groups)
        remote(half.at[p], recv.at[place], main_rs, device(2 * p + core)).start()

    recv[place] = half[place]

    feature_rows(2, 6)
    wait_bytes(recv.at[others], main_rs.at[1])

    def add(i, total):
        return total + recv[i].astype(F32)

    total = lax.fori_loop(0, groups, add, jnp.zeros(recv.shape[1:], F32))
    gath[core, place] = rounded(total)

    @pl.loop(1, groups)
    def _(d):
        p = lax.rem(place + d, groups)
        pltpu.make_async_remote_copy(
            src_ref=gath.at[core, place], dst_ref=gath.at[core, place], send_sem=ag_send,
            recv_sem=ag_recv.at[place], device_id=device(2 * p + core),
            device_id_type=pl.DeviceIdType.MESH,
        ).start()

    remote(gath.at[core, place], gath.at[core, place], pair_ag, partner).start()
    feature_rows(6, rows)
    for c in range(width // 128):
        part = own32[pl.ds(c * channels * rows, channels * rows), :]
        out_ref[:, :, 128 * c : 128 * c + 128] = part.reshape(channels, rows, 128).astype(BF16)

    @pl.loop(1, groups)
    def _(d):
        p = lax.rem(place + groups - d, groups)
        wait_bytes(gath.at[core, p], ag_recv.at[p])
        remote(gath.at[core, p], gath.at[core, p], pair_ag, partner).start()

    wait_bytes(gath.at[1 - core], pair_ag.at[1])

    gath_out[...] = gath[...]

    @pl.when(has_hi)
    def _():
        for copy in to_next():
            copy.wait_send()

    @pl.when(has_lo)
    def _():
        for copy in to_previous():
            copy.wait_send()

    @pl.when(owner)
    def _():
        wait_bytes(gram.at[pl.ds(0, owners - 1)], gram_rs.at[0])
        wait_bytes(gram_recv.at[rest], gram_ag.at[0])

    @pl.when(jnp.logical_not(owner))
    def _():
        wait_bytes(gram, gram_rs.at[0])

    swap.wait_send()
    wait_bytes(recv.at[others], main_rs.at[0])
    wait_bytes(half.at[others], ag_send)
    wait_bytes(gath.at[core], pair_ag.at[0])


def finish_kernel(
    adjoint_ref, gath_ref, mixer_t, scale_ref, offset_ref,
    out_ref, triple_ref, stencil_ref, outgoing_ref, sharp_ref, scaling_ref, offset_out_ref, sem,
):
    move = pltpu.make_async_copy(adjoint_ref, out_ref, sem)
    move.start()
    channels, n1 = mixer_t.shape
    n2 = n1 + channels
    left = gath_ref[0].reshape(-1, 128).astype(F32)
    right = gath_ref[1].reshape(-1, 128).astype(F32)
    full = right + pltpu.roll(right, 96, 1)
    s = jnp.concatenate([left[0:n1], right[0:n1, 0:64]], axis=1)
    gsum = full[0:n1, 64:65]
    triple_ref[...] = (s * scale_ref[...] + gsum * offset_ref[...]).T
    turned = full[0:n1].T
    for t in range(9):
        stencil_ref[t // 3, t % 3 : t % 3 + 1, :] = turned[72 + t : 73 + t, :]
    outgoing_ref[...] = jnp.concatenate([left[n1:n2], right[n1:n2, 0:64]], axis=1)
    sharp_ref[...] = full[n1 : n1 + 1, 64:68]
    scaling_ref[...] = full[n1:n2].T[72:73, :]
    mixer = mixer_t[...].T.astype(F32)
    offset_out_ref[...] = jnp.sum(mixer * gsum, axis=0, keepdims=True)
    move.wait()


def local(
    block_feature_map, upstream_sensitivity, triple_mixer, spatial_stencil, outgoing_mixer,
    sharpness_factor, standardize_scaling, standardize_offset,
):
    _, channels, rows, width = block_feature_map.shape
    n_img = lax.axis_size("img")
    n_tile = lax.axis_size("tile")
    groups = n_img * n_tile // 2
    n1 = 3 * channels
    each = -(-channels // (n_tile * 8)) * 8
    owners = -(-channels // each)
    piece = -(-4 * channels // (groups * 16)) * 16

    shape = jax.ShapeDtypeStruct
    vmem = pltpu.VMEM
    pair_sem = pltpu.SemaphoreType.DMA((2,))
    mixer_t = triple_mixer.T
    scale_row = standardize_scaling.reshape(1, channels)
    offset_row = standardize_offset.reshape(1, channels)
    adjoint, gathered = pl.pallas_call(
        functools.partial(kernel, n_img, n_tile),
        out_shape=(
            shape((channels, rows, width), BF16),
            shape((2, groups, piece, 128), BF16),
        ),
        in_specs=[VMEM] * 7 + [SMEM],
        out_specs=[VMEM] * 2,
        scratch_shapes=[
            vmem((4, channels, 128), F32),
            vmem((channels * rows * width // 128, 128), F32),
            vmem((channels * rows * width // 128, 128), F32),
            vmem((rows, channels, width), F32),
            vmem((rows, 256, width), BF16),
            vmem((rows, 1, width), F32),
            vmem((rows, channels, width), BF16),
            vmem((rows, channels, width), BF16),
            vmem((n1, channels), BF16),
            vmem((channels, channels), BF16),
            vmem((n1, 128), F32),
            vmem((3, channels, width), BF16),
            vmem((3, channels, width), BF16),
            vmem((rows + 4, n1, width), BF16),
            vmem((rows + 2, n1, width), BF16),
            vmem((rows + 2, channels, width), BF16),
            vmem((rows + 2, n1, width), BF16),
            vmem((rows, n1, width), BF16),
            vmem((5, channels, 256), F32),
            vmem((owners, each, 128), F32),
            vmem((n_tile, each, 128), F32),
            vmem((owners, each, 128), F32),
            vmem((channels, channels), BF16),
            vmem((channels, channels), BF16),
            vmem((channels, channels), BF16),
            vmem((channels, 128), F32),
            vmem((n1, 256), F32),
            vmem((4 * channels, 128), F32),
            vmem((2, groups, piece, 128), BF16),
            vmem((groups, piece, 128), BF16),
            vmem((groups, piece, 128), BF16),
            vmem((groups, piece, 128), BF16),
            vmem((2, groups, piece, 128), BF16),
        ]
        + [pair_sem] * 9
        + [pltpu.SemaphoreType.DMA, pltpu.SemaphoreType.DMA((groups,))],
        compiler_params=pltpu.CompilerParams(
            collective_id=0, has_side_effects=True, vmem_limit_bytes=LIMIT
        ),
        name="block",
    )(
        block_feature_map[0], upstream_sensitivity[0], mixer_t,
        jnp.transpose(spatial_stencil, (1, 2, 0)), outgoing_mixer, scale_row, offset_row,
        sharpness_factor,
    )
    anywhere = pl.BlockSpec(memory_space=pl.ANY)
    out, triple, stencil, outgoing, sharp, scaling, offset = pl.pallas_call(
        finish_kernel,
        out_shape=(
            shape((channels, rows, width), BF16),
            shape((channels, n1), F32),
            shape((3, 3, n1), F32),
            shape((channels, channels), F32),
            shape((1, sharpness_factor.shape[0]), F32),
            shape((1, channels), F32),
            shape((1, channels), F32),
        ),
        in_specs=[anywhere] + [VMEM] * 4,
        out_specs=[anywhere] + [VMEM] * 6,
        scratch_shapes=[pltpu.SemaphoreType.DMA],
        compiler_params=pltpu.CompilerParams(vmem_limit_bytes=LIMIT),
        name="finish",
    )(adjoint, gathered, mixer_t, scale_row, offset_row)
    return (
        out[None],
        triple.T,
        jnp.transpose(stencil, (2, 0, 1)),
        outgoing,
        sharp[0],
        scaling[0],
        offset[0],
    )


def solution(mesh):
    rows = P("img", None, "tile", None)
    return jax.shard_map(
        local,
        mesh=mesh,
        in_specs=(rows, rows, P(), P(), P(), P(), P(), P()),
        out_specs=(rows, P(), P(), P(), P(), P(), P()),
        check_vma=False,
    )
```
